32 devices in a mesh: ctx: 8 (over y, x, core), exp: 4 (over z).
Axes of the slice: x: 2, y: 2, z: 4, core: 2. Of those that a mesh axis runs over, the one named last changes fastest.
Arguments:
- queries: bfloat16 [1024, 6144], P('ctx', 'exp'), may hold values from -0.71875 to 0.71875
- keys: bfloat16 [1024, 6144], P('ctx', 'exp'), may hold values from -0.71875 to 0.71875
- values: bfloat16 [1024, 6144], P('ctx', 'exp'), may hold values from -0.71875 to 0.71875
- out_grad: bfloat16 [1024, 6144], P('ctx', 'exp'), may hold values from -0.71875 to 0.71875
- log_decay: float32 [1024, 48], P('ctx', 'exp'), may hold values from -1.6 to 0, as said below
- moe_grad: bfloat16 [1024, 6144], P('ctx', 'exp'), may hold values from -6 to 6
- expert_ids: int32 [1024, 2], P('ctx'), may hold values from 0 to 3, all different within a row; in each aligned block of 128 rows (0 to 127, 128 to 255, ...) at most 80 rows name the same one
- gate_weights: float32 [1024, 2], P('ctx'), may hold values from 0.2 to 1
- down_weight: bfloat16 [8, 3072, 6144], P('ctx', 'exp'), may hold values from -0.078125 to 0.078125
Outputs:
- query_grad: bfloat16 [1024, 6144], P('ctx', 'exp')
- key_grad: bfloat16 [1024, 6144], P('ctx', 'exp')
- value_grad: bfloat16 [1024, 6144], P('ctx', 'exp')
- hidden_grad: bfloat16 [8, 640, 3072], P('ctx', None, 'exp')
The draws below stay inside these ranges and needn't reach their ends.
Inputs may be any that keep to these rules, and one draw needn't show every extreme that they name: `expert_ids`: in the rows of one device (aligned blocks of 128 tokens) no expert is named more than 80 times, and in every draw some expert is named exactly 80 times in some block; a token's two experts differ. `log_decay`: every entry is negative.
All inputs are finite; a program needn't handle non-finite values.
Results may differ from the reference program's by a relative error of at most 0.0049.
Values may be sent and summed in bfloat16 or wider, within the bound.
A program may use at most 128 MiB of HBM per device.

```python
import math
import jax
import jax.numpy as jnp
import numpy as np
from jax import lax

D = 6144
FF = 6144
HEAD_TOTAL = 48
HD = 128
TOK_DEV = 128
EXPERTS = 4
CAP = 80
TOKEN_TOTAL = 1024


def draw_log_decay(key, part):
    folded = jax.random.fold_in(key, 7)
    pick_key, slow_key, fast_key, rough_key, location_random_key, loss_random_key = jax.random.split(folded, 6)
    fast_share = 0.5
    is_fast = jax.random.uniform(pick_key, (HEAD_TOTAL,)) < fast_share
    slow_rate = jnp.exp(jax.random.uniform(slow_key, (HEAD_TOTAL,), minval=jnp.log(0.2), maxval=jnp.log(0.8))) / TOKEN_TOTAL
    fast_rate = jnp.exp(jax.random.uniform(fast_key, (HEAD_TOTAL,), minval=jnp.log(1.0 / 50.0), maxval=jnp.log(1.0 / 30.0)))
    decay_factor = jnp.where(is_fast, fast_rate, slow_rate)
    jaggedness = jax.random.uniform(rough_key, (TOKEN_TOTAL, HEAD_TOTAL), minval=0.5, maxval=1.5)
    spike_locations = jax.random.randint(location_random_key, (2, HEAD_TOTAL), 0, TOKEN_TOTAL)
    spike_loss = jnp.log(jax.random.uniform(loss_random_key, (2, HEAD_TOTAL), minval=0.5, maxval=0.8))
    position_indices = jnp.arange(TOKEN_TOTAL)[:, None, None] == spike_locations[None]
    spike_total_sum = jnp.sum(jnp.where(position_indices, spike_loss[None], 0.0), axis=1)
    return (-decay_factor[None, :] * jaggedness + spike_total_sum).astype(jnp.float32)


def steps_of(rng, extent, shards, low, top_value):
    factor_of = 1.0
    for position, parts in shards:
        steps = jax.random.uniform(jax.random.fold_in(jax.random.fold_in(rng, 6), position), (parts,), jnp.float32, low / len(shards), top_value / len(shards))
        factor_of = factor_of * jnp.repeat(jnp.exp(steps), extent[position] // parts).reshape((-1,) + (1,) * (len(extent) - 1 - position))
    return factor_of


def deal_out(own_key, own, number, rows, amount, top, limit, slope):
    ranking = jax.random.permutation(own_key, amount)
    heavy_load, common = shares(amount, rows * top, limit, slope, True), shares(amount, rows * top, limit, slope, False)
    places = jnp.arange(amount)

    def named(tallies, offset_by):
        used = int((tallies > 0).sum())
        fixed = max(1, used // 4)
        moved = fixed + (places - fixed + offset_by * (used - fixed)) % max(1, amount - fixed)
        return jnp.zeros((amount,), jnp.int32).at[ranking[jnp.where(places < fixed, places, moved)]].set(jnp.asarray(tallies, jnp.int32))

    tallies = jnp.where(number % 4 == 0, named(heavy_load, number // 4), named(common, number - number // 4 - 1))
    mixed = jax.random.permutation(jax.random.fold_in(own, 3), amount)
    giver, sink = mixed[0:amount // 2 * 2:2], mixed[1:amount // 2 * 2:2]
    margin = jnp.minimum(tallies[giver] - 1, limit - tallies[sink]) // 2
    margin = jnp.where((giver == ranking[0]) | (sink == ranking[0]) | (tallies[sink] == 0), 0, jnp.maximum(margin, 0))
    moved = jax.random.randint(jax.random.fold_in(own, 4), (amount // 2,), 0, 1 << 20) % (margin + 1)
    tallies = tallies.at[giver].add(-moved).at[sink].add(moved)
    labels = jnp.searchsorted(jnp.cumsum(tallies), jnp.arange(rows * top), side="right").astype(jnp.int32)
    listing = labels.reshape(top, rows).T
    listing = listing[jax.random.permutation(jax.random.fold_in(own, 1), rows)]
    offset_by = jax.random.randint(jax.random.fold_in(own, 2), (rows, 1), 0, top)
    return jnp.take_along_axis(listing, (jnp.arange(top)[None, :] + offset_by) % top, axis=1)


def shares(amount, total, bound, slope, full):
    weights = [(1 << 20) // math.isqrt(rank ** slope) + 1 for rank in range(1, amount + 1)]
    largest = bound if full else min(bound, max(-(-total // amount), total * weights[0] // sum(weights)))
    least = 1 if total - largest >= amount - 1 else 0
    given, surplus = [largest] + [least] * (amount - 1), total - largest - least * (amount - 1)
    while surplus > 0:
        candidates = [i for i in range(1, amount) if given[i] < largest] or [i for i in range(1, amount) if given[i] < bound]
        pool, budget = sum([weights[i] for i in candidates]), surplus
        for i in candidates:
            more = min(bound - given[i], max(1, budget * weights[i] // pool), surplus)
            given[i] = given[i] + more
            surplus = surplus - more
    return np.array(given)


def noise(rng, shape, deviation, bound, cuts=(), dtype=jnp.bfloat16):
    loudness = steps_of(rng, shape, cuts, -0.22, 0.18) if cuts else 1.0
    entries = jax.random.normal(rng, shape, jnp.float32) * deviation * loudness
    return jnp.minimum(jnp.maximum(entries, -bound), bound).astype(dtype)


def setup_inputs(seed: int = 0) -> dict:
    splits = jax.random.split(jax.random.key(seed), 10)
    queries = noise(splits[0], (TOKEN_TOTAL, HEAD_TOTAL * HD), 0.12, 0.71875, ((0, 8), (1, 4)))
    keys = noise(splits[1], (TOKEN_TOTAL, HEAD_TOTAL * HD), 0.12, 0.71875, ((0, 8), (1, 4)))
    values = noise(splits[2], (TOKEN_TOTAL, HEAD_TOTAL * HD), 0.12, 0.71875, ((0, 8), (1, 4)))
    out_grad = noise(splits[3], (TOKEN_TOTAL, HEAD_TOTAL * HD), 0.12, 0.71875, ((0, 8), (1, 4)))
    log_decay = draw_log_decay(jax.random.fold_in(splits[9], 71), 0)
    moe_grad = noise(splits[5], (TOKEN_TOTAL, D), 1.0, 6.0, ((0, 8), (1, 4)))
    expert_ids_keys = jax.random.split(jax.random.fold_in(splits[6], 1), TOKEN_TOTAL // TOK_DEV)
    expert_ids_turns = jax.random.permutation(jax.random.fold_in(splits[6], 3), TOKEN_TOTAL // TOK_DEV)
    expert_ids = jax.vmap(lambda own, number: deal_out(jax.random.fold_in(splits[6], 2), own, number, TOK_DEV, EXPERTS, 2, CAP, 1))(expert_ids_keys, expert_ids_turns).reshape((TOKEN_TOTAL, 2))
    gate_weights = jnp.clip(0.2 + 0.8 * jax.random.uniform(splits[7], (TOKEN_TOTAL, 2), jnp.float32) ** steps_of(splits[7], (TOKEN_TOTAL, 2), ((0, 8),), -0.2, 0.2), 0.2, 1.0)
    down_weight = noise(splits[8], (2 * EXPERTS, FF // 2, D), FF ** -0.5, 0.078125, ((0, 8), (1, 4)))
    return dict(queries=queries, keys=keys, values=values, out_grad=out_grad, log_decay=log_decay, moe_grad=moe_grad, expert_ids=expert_ids, gate_weights=gate_weights, down_weight=down_weight)


def head_grads(inputs):
    query_h, key_h, value_h, grad_h, decay_h = inputs
    running = jnp.cumsum(decay_h, axis=1)
    closing = running[:, -1]
    length = running.shape[1]
    causal = jnp.arange(length)[:, None] >= jnp.arange(length)[None, :]
    spread = running[:, :, None] - running[:, None, :]
    weights = jnp.where(causal[None], jnp.exp(jnp.where(causal[None], spread, 0.0)), 0.0)
    query_full = query_h.astype(jnp.float32)
    key_full = key_h.astype(jnp.float32)
    value_full = value_h.astype(jnp.float32)
    gradient_full = grad_h.astype(jnp.float32)
    until_finish = jnp.exp(closing[:, None] - running)
    since_beginning = jnp.exp(running)
    block_state = jnp.einsum("bsk,bsv->bkv", key_full * until_finish[:, :, None], value_full, precision=lax.Precision.HIGHEST)
    block_grad = jnp.einsum("btk,btv->bkv", query_full * since_beginning[:, :, None], gradient_full, precision=lax.Precision.HIGHEST)
    block_decay = jnp.exp(closing)

    def forward_step(carried, block_item):
        state_in, decay_in = block_item
        return decay_in * carried + state_in, carried

    zero_state = jnp.zeros(block_state.shape[1:], jnp.float32)
    _, leading_part = lax.scan(forward_step, zero_state, (block_state, block_decay))
    _, trailing_part = lax.scan(forward_step, zero_state, (block_grad, block_decay), reverse=True)
    grad_scores = (jnp.einsum("btv,bsv->bts", gradient_full, value_full) * weights).astype(jnp.bfloat16)
    grad_scores = lax.optimization_barrier(grad_scores).astype(jnp.float32)
    scores = (jnp.einsum("btk,bsk->bts", query_full, key_full) * weights).astype(jnp.bfloat16)
    scores = lax.optimization_barrier(scores).astype(jnp.float32)
    query_grad = jnp.einsum("bts,bsk->btk", grad_scores, key_full) + since_beginning[:, :, None] * jnp.einsum("btv,bkv->btk", gradient_full, leading_part, precision=lax.Precision.HIGHEST)
    key_grad = jnp.einsum("bts,btk->bsk", grad_scores, query_full) + until_finish[:, :, None] * jnp.einsum("bsv,bkv->bsk", value_full, trailing_part, precision=lax.Precision.HIGHEST)
    value_grad = jnp.einsum("bts,btv->bsv", scores, gradient_full) + until_finish[:, :, None] * jnp.einsum("bsk,bkv->bsv", key_full, trailing_part, precision=lax.Precision.HIGHEST)
    return (query_grad.astype(jnp.bfloat16), key_grad.astype(jnp.bfloat16), value_grad.astype(jnp.bfloat16))


def reference(queries, keys, values, out_grad, log_decay, moe_grad, expert_ids, gate_weights, down_weight):
    blocks = TOKEN_TOTAL // TOK_DEV

    def per_head(stacked):
        return stacked.reshape(blocks, TOK_DEV, HEAD_TOTAL, HD).transpose(2, 0, 1, 3)

    def merge_heads(stacked):
        return stacked.transpose(1, 2, 0, 3).reshape(TOKEN_TOTAL, HEAD_TOTAL * HD)

    decay_heads = log_decay.reshape(blocks, TOK_DEV, HEAD_TOTAL).transpose(2, 0, 1)
    outputs = lax.map(head_grads, (per_head(queries), per_head(keys), per_head(values), per_head(out_grad), decay_heads))
    query_grad = merge_heads(outputs[0])
    key_grad = merge_heads(outputs[1])
    value_grad = merge_heads(outputs[2])

    pair_ids = expert_ids.reshape(blocks, 2 * TOK_DEV)
    pair_gates = gate_weights.reshape(blocks, 2 * TOK_DEV)
    onehot = (pair_ids[:, :, None] == jnp.arange(EXPERTS)[None, None, :]).astype(jnp.int32)
    earlier = jnp.cumsum(onehot, axis=1) - onehot
    pair_ranks = jnp.sum(earlier * onehot, axis=2)
    pair_slots = pair_ids * CAP + pair_ranks
    grad_blocks = moe_grad.reshape(blocks, TOK_DEV, D)

    def route_block(inputs):
        slot_row, gate_row, grad_rows = inputs
        dispatch_table = (jnp.arange(EXPERTS * CAP)[:, None] == slot_row[None, :]).astype(jnp.float32) * gate_row[None, :]
        dispatch_table = dispatch_table.reshape(EXPERTS * CAP, TOK_DEV, 2).sum(axis=2)
        return jnp.dot(dispatch_table, grad_rows.astype(jnp.float32), precision=lax.Precision.HIGHEST).astype(jnp.bfloat16)

    routed = lax.map(route_block, (pair_slots, pair_gates, grad_blocks))
    routed = routed.reshape(blocks, EXPERTS, CAP, D).transpose(1, 0, 2, 3).reshape(EXPERTS, blocks * CAP, D)
    halves = down_weight.reshape(EXPERTS, FF, D)

    def expert_block(inputs):
        expert_rows, expert_weight = inputs
        product = jnp.dot(expert_rows, expert_weight.T, preferred_element_type=jnp.float32).astype(jnp.bfloat16)
        return product.reshape(blocks * CAP, 2, FF // 2).transpose(1, 0, 2)

    hidden_grad = lax.map(expert_block, (routed, halves)).reshape(2 * EXPERTS, blocks * CAP, FF // 2)
    return (query_grad, key_grad, value_grad, hidden_grad)
```

```python
import functools

import jax
import jax.numpy as jnp
from jax import lax
from jax.experimental import pallas as pl
from jax.experimental.pallas import tpu as pltpu
from jax.sharding import PartitionSpec as P


def carried_in(x, axis, combine, identity, reverse):
    devices, place = (lax.axis_size(axis), lax.axis_index(axis))
    everything = jax.tree.map(lambda part: lax.all_gather(part, axis), x)
    start = jax.tree.map(
        lambda part, zero: jnp.broadcast_to(jnp.asarray(zero, part.dtype), part.shape), x, identity
    )

    def turn(k, before):
        at = devices - 1 - k if reverse else k
        reached = at > place if reverse else at < place
        new = combine(before, jax.tree.map(lambda part: part[at], everything))
        return jax.tree.map(lambda a, b: jnp.where(reached, a, b), new, before)

    return lax.fori_loop(0, devices, turn, start)


def partner_2(value, axis, apart):
    mask = 2**apart
    pairs = [(source, source ^ mask) for source in range(lax.axis_size(axis))]
    return lax.ppermute(value, axis, pairs)


def combine_states(earlier, later):
    return (later[1][:, None, None] * earlier[0] + later[0], earlier[1] * later[1])


def attention_grads(queries, keys, values, out_grad, log_decay):
    length, head_count = log_decay.shape
    head_size = queries.shape[1] // head_count
    query_h = queries.reshape(length, head_count, head_size)
    key_h = keys.reshape(length, head_count, head_size)
    value_h = values.reshape(length, head_count, head_size)
    grad_h = out_grad.reshape(length, head_count, head_size)
    running = jnp.cumsum(log_decay, axis=0)
    closing = running[-1]
    causal = jnp.arange(length)[:, None] >= jnp.arange(length)[None, :]
    spread = running.T[:, :, None] - running.T[:, None, :]
    weights = jnp.where(causal[None], jnp.exp(jnp.where(causal[None], spread, 0.0)), 0.0)
    until_finish = jnp.exp(closing[None, :] - running)
    since_beginning = jnp.exp(running)
    query_full = query_h.astype(jnp.float32)
    key_full = key_h.astype(jnp.float32)
    value_full = value_h.astype(jnp.float32)
    gradient_full = grad_h.astype(jnp.float32)
    block_state = jnp.einsum(
        "jqz,jqb->qzb",
        key_full * until_finish[:, :, None],
        value_full,
        precision=lax.Precision.HIGHEST,
    )
    block_grad = jnp.einsum(
        "soj,sop->ojp",
        query_full * since_beginning[:, :, None],
        gradient_full,
        precision=lax.Precision.HIGHEST,
    )
    block_decay = jnp.exp(closing)
    identity_pair = (jnp.zeros_like(block_state), jnp.ones_like(block_decay))
    leading_part, _ = carried_in(
        (block_state, block_decay), "ctx", combine_states, identity_pair, False
    )
    trailing_part, _ = carried_in(
        (block_grad, block_decay), "ctx", combine_states, identity_pair, True
    )
    grad_scores = (
        jnp.einsum("thv,shv->hts", grad_h, value_h, preferred_element_type=jnp.float32) * weights
    ).astype(jnp.bfloat16)
    scores = (
        jnp.einsum("thk,shk->hts", query_h, key_h, preferred_element_type=jnp.float32) * weights
    ).astype(jnp.bfloat16)
    query_grad = jnp.einsum(
        "hts,shk->thk", grad_scores, key_h, preferred_element_type=jnp.float32
    ) + since_beginning[:, :, None] * jnp.einsum(
        "xrq,rgq->xrg", gradient_full, leading_part, precision=lax.Precision.HIGHEST
    )
    key_grad = jnp.einsum(
        "hts,thk->shk", grad_scores, query_h, preferred_element_type=jnp.float32
    ) + until_finish[:, :, None] * jnp.einsum(
        "pox,ofx->pof", value_full, trailing_part, precision=lax.Precision.HIGHEST
    )
    value_grad = jnp.einsum(
        "hts,thv->shv", scores, grad_h, preferred_element_type=jnp.float32
    ) + until_finish[:, :, None] * jnp.einsum(
        "raj,ajb->rab", key_full, trailing_part, precision=lax.Precision.HIGHEST
    )
    flat_width = head_count * head_size
    return (
        query_grad.reshape(length, flat_width).astype(jnp.bfloat16),
        key_grad.reshape(length, flat_width).astype(jnp.bfloat16),
        value_grad.reshape(length, flat_width).astype(jnp.bfloat16),
    )


def route_rows(moe_grad, expert_ids, gate_weights, experts, capacity):
    pair_ids = expert_ids.reshape(-1)
    onehot = (pair_ids[:, None] == jnp.arange(experts)[None, :]).astype(jnp.int32)
    earlier = jnp.cumsum(onehot, axis=0) - onehot
    pair_slots = (pair_ids * capacity + jnp.sum(earlier * onehot, axis=1)).reshape(-1, 2)
    slot_iota = jnp.arange(experts * capacity)[:, None]
    first_table = jnp.where(
        slot_iota == pair_slots[:, 0][None, :], gate_weights[:, 0][None, :], 0.0
    )
    second_table = jnp.where(
        slot_iota == pair_slots[:, 1][None, :], gate_weights[:, 1][None, :], 0.0
    )
    dispatch_table = first_table + second_table
    return jnp.dot(
        dispatch_table, moe_grad.astype(jnp.float32), precision=lax.Precision.HIGHEST
    ).astype(jnp.bfloat16)


def per_device(
    queries, keys, values, out_grad, log_decay, moe_grad, expert_ids, gate_weights, down_weight
):
    query_grad, key_grad, value_grad = attention_grads(queries, keys, values, out_grad, log_decay)
    devices_ctx = lax.axis_size("ctx")
    experts = devices_ctx // 2
    length = moe_grad.shape[0]
    capacity = 5 * length // (2 * experts)
    routed = route_rows(moe_grad, expert_ids, gate_weights, experts, capacity)
    weight_slab = down_weight[0]
    half_count = capacity // 2
    own_rows = lax.all_to_all(routed, "ctx", split_axis=0, concat_axis=0, tiled=True)
    own_full = lax.all_gather(own_rows, "exp", axis=1, tiled=True)
    partner = partner_2(own_full, "ctx", 0)
    parity = lax.axis_index("ctx") % 2
    own_view = own_full.reshape(devices_ctx, half_count, -1)
    partner_view = partner.reshape(devices_ctx, half_count, -1)
    lower_half = jnp.where(parity == 0, own_view, partner_view)
    upper_half = jnp.where(parity == 0, partner_view, own_view)
    all_rows = jnp.concatenate([lower_half, upper_half], axis=1).reshape(devices_ctx * capacity, -1)
    hidden = jnp.einsum("sd,fd->sf", all_rows, weight_slab, preferred_element_type=jnp.float32)
    hidden_grad = hidden.astype(jnp.bfloat16)[None]
    return (query_grad, key_grad, value_grad, hidden_grad)


MESH = pl.DeviceIdType.MESH
NT = (((1,), (1,)), ((), ()))
NN = (((1,), (0,)), ((), ()))
TN = (((0,), (0,)), ((), ()))


def mm(a, b, dims, precision=None):
    return lax.dot_general(a, b, dims, precision=precision, preferred_element_type=jnp.float32)


def split_bf16(x):
    high = x.astype(jnp.bfloat16)
    return high, (x - high.astype(jnp.float32)).astype(jnp.bfloat16)


def causal_mask(size):
    return lax.broadcasted_iota(jnp.int32, (size, size), 0) >= lax.broadcasted_iota(
        jnp.int32, (size, size), 1
    )


def fused_kernel(
    sizes,
    q_ref,
    k_ref,
    v_ref,
    g_ref,
    ld_ref,
    moe_ref,
    ids_ref,
    gate_ref,
    w_hbm,
    qg_ref,
    kg_ref,
    vg_ref,
    hid_ref,
    wbuf,
    raw,
    sendbuf,
    rows,
    acc,
    table,
    slot_gate,
    run_col,
    run_row,
    close_row,
    own_decay,
    sib_decay,
    chip_decay,
    far_decay,
    state,
    sib_state,
    chip_state,
    far_state,
    pair_state,
    y_state,
    outer,
    local,
    w_sem,
    own_send,
    fwd_send,
    raw_recv,
    xy_send,
    xy_recv,
    sib_send,
    sib_recv,
    lvl_send,
    lvl_recv,
):
    n_z, n_chip, cap, heads, size = sizes
    half = heads // 2
    length = moe_ref.shape[0]
    width = moe_ref.shape[1]
    c, z = lax.axis_index("ctx"), lax.axis_index("exp")
    core = c % 2
    chip = c // 2
    xbit, ybit = chip % 2, chip // 2
    sib = c + 1 - 2 * core
    xpart = c + 2 - 4 * xbit
    ypart = c + 4 - 8 * ybit
    has_left, has_right = z > 0, z < n_z - 1

    def chip_at(d):
        return (chip + d) % n_chip

    barrier = pltpu.get_barrier_semaphore()
    for d in range(1, n_chip):
        pl.semaphore_signal(
            barrier, inc=1, device_id={"ctx": chip_at(d) * 2 + core}, device_id_type=MESH
        )
    pl.semaphore_signal(barrier, inc=1, device_id={"ctx": sib}, device_id_type=MESH)

    @pl.when(has_left)
    def _():
        pl.semaphore_signal(barrier, inc=1, device_id={"exp": z - 1}, device_id_type=MESH)

    @pl.when(has_right)
    def _():
        pl.semaphore_signal(barrier, inc=1, device_id={"exp": z + 1}, device_id_type=MESH)

    line_peers = jnp.minimum(z, 1) + jnp.minimum(n_z - 1 - z, 1)
    pl.semaphore_wait(barrier, n_chip + line_peers)

    def own_copy(side):
        return pltpu.make_async_remote_copy(
            src_ref=moe_ref,
            dst_ref=raw.at[z],
            send_sem=own_send.at[side],
            recv_sem=raw_recv.at[z],
            device_id={"exp": z - 1 + 2 * side},
            device_id_type=MESH,
        )

    @pl.when(has_left)
    def _():
        own_copy(0).start()

    @pl.when(has_right)
    def _():
        own_copy(1).start()

    w_copies = [
        pltpu.make_async_copy(w_hbm.at[0, :, pl.ds(i * width, width)], wbuf.at[i], w_sem.at[i])
        for i in range(n_z)
    ]
    for copy in w_copies:
        copy.start()

    mirrored = jnp.where(2 * z < n_z, z, n_z - 1 - z)

    def chunk_at(i):
        if i == 0:
            return z
        near = mirrored + (i + 1) // 2 if i % 2 else mirrored - i // 2
        from_low = jnp.where(i <= 2 * mirrored, near, i)
        return jnp.where(2 * z < n_z, from_low, n_z - 1 - from_low)

    ids = ids_ref[...]
    gates = gate_ref[...]
    expert = lax.broadcasted_iota(jnp.int32, (length, 128), 1)
    first, second = ids[:, 0:1] == expert, ids[:, 1:2] == expert
    named = (first | second).astype(jnp.float32)
    weight = jnp.where(first, gates[:, 0:1], 0.0) + jnp.where(second, gates[:, 1:2], 0.0)
    t_row = lax.broadcasted_iota(jnp.int32, (length, length), 0)
    t_col = lax.broadcasted_iota(jnp.int32, (length, length), 1)
    earlier = (t_row < t_col).astype(jnp.float32)
    rank_row = mm(named, earlier, TN)
    named_row = named.T
    weight_row = weight.T
    slot = lax.broadcasted_iota(jnp.int32, (cap, length), 0).astype(jnp.float32)
    for e in range(n_chip):
        hit = (rank_row[e : e + 1, :] == slot) & (named_row[e : e + 1, :] > 0.5)
        table[e] = hit.astype(jnp.float32).astype(jnp.bfloat16)
        gate = jnp.sum(jnp.where(hit, weight_row[e : e + 1, :], 0.0), axis=1, keepdims=True)
        slot_gate[e] = jnp.broadcast_to(gate, (cap, 128))

    def xy_copy(i, s, d):
        return pltpu.make_async_remote_copy(
            src_ref=sendbuf.at[i, d - 1],
            dst_ref=rows.at[s, c],
            send_sem=xy_send.at[i, d],
            recv_sem=xy_recv.at[s, chip],
            device_id={"ctx": chip_at(d) * 2 + core},
            device_id_type=MESH,
        )

    def xy_arrival(i, s, d):
        source = chip_at(d)
        return pltpu.make_async_remote_copy(
            src_ref=sendbuf.at[i, d - 1],
            dst_ref=rows.at[s, source * 2 + core],
            send_sem=xy_send.at[i, d],
            recv_sem=xy_recv.at[s, source],
            device_id={"ctx": source * 2 + core},
            device_id_type=MESH,
        )

    def sib_copy(s, d):
        block = rows.at[s, chip_at(d) * 2 + core]
        return pltpu.make_async_remote_copy(
            src_ref=block,
            dst_ref=block,
            send_sem=sib_send.at[s, d],
            recv_sem=sib_recv.at[s, d],
            device_id={"ctx": sib},
            device_id_type=MESH,
        )

    def sib_arrival(s, d):
        block = rows.at[s, chip_at(d) * 2 + 1 - core]
        return pltpu.make_async_remote_copy(
            src_ref=block,
            dst_ref=block,
            send_sem=sib_send.at[s, d],
            recv_sem=sib_recv.at[s, d],
            device_id={"ctx": sib},
            device_id_type=MESH,
        )

    def forward_copy(i, s, side):
        return pltpu.make_async_remote_copy(
            src_ref=raw.at[s],
            dst_ref=raw.at[s],
            send_sem=fwd_send.at[i],
            recv_sem=raw_recv.at[s],
            device_id={"exp": z - 1 + 2 * side},
            device_id_type=MESH,
        )

    def forwards(s):
        return (s < z) & has_right, (s > z) & has_left

    def route_chunk(i):
        s = chunk_at(i)
        if i:
            pltpu.make_async_remote_copy(
                src_ref=raw.at[s],
                dst_ref=raw.at[s],
                send_sem=fwd_send.at[i],
                recv_sem=raw_recv.at[s],
                device_id={"exp": s},
                device_id_type=MESH,
            ).wait_recv()
            to_right, to_left = forwards(s)

            @pl.when(to_right)
            def _():
                forward_copy(i, s, 1).start()

            @pl.when(to_left)
            def _():
                forward_copy(i, s, 0).start()

        for d in (*range(1, n_chip), 0):
            e = chip_at(d)
            picked = mm(table[e], raw[s] if i else moe_ref[...], NN)
            routed = (picked * slot_gate[e][:, 0:1]).astype(jnp.bfloat16)
            if d:
                sendbuf[i, d - 1] = routed
                xy_copy(i, s, d).start()
            else:
                rows[s, c] = routed
                sib_copy(s, 0).start()

    def pass_on(i):
        s = chunk_at(i)
        for d in range(1, n_chip):
            xy_arrival(i, s, d).wait_recv()
            sib_copy(s, d).start()

    def multiply(i):
        s = chunk_at(i)
        for d in range(n_chip):
            sib_arrival(s, d).wait_recv()
        if i == 0:
            for copy in w_copies:
                copy.wait()

        def tile(j, carry):
            left = rows[s, pl.ds(2 * j, 2)].reshape(2 * cap, width)
            part = mm(left, wbuf[s], NT)
            if i:
                part = part + acc[j]
            if i < n_z - 1:
                acc[j] = part
            else:
                hid_ref[0, pl.ds(pl.multiple_of(j * 2 * cap, 2 * cap), 2 * cap), :] = part.astype(
                    jnp.bfloat16
                )
            return carry

        lax.fori_loop(0, n_chip, tile, 0)

    route_chunk(0)

    log_decay = ld_ref[...]
    highest = lax.Precision.HIGHEST
    lower = (t_row >= t_col).astype(jnp.float32)
    upper = (t_row <= t_col).astype(jnp.float32)
    running = mm(lower, log_decay, NN, highest)
    running_t = mm(log_decay, upper, TN, highest)
    closing = mm(log_decay, jnp.ones((length, size), jnp.float32), TN, highest)
    for h in range(heads):
        run_col[h] = jnp.broadcast_to(running[:, h : h + 1], (length, size))
        run_row[h] = jnp.broadcast_to(running_t[h : h + 1, :], (8, length))
        close_row[h] = jnp.broadcast_to(closing[h : h + 1, :], (8, size))
        own_decay[h] = jnp.broadcast_to(jnp.exp(closing[h : h + 1, :]), (8, size))

    group = 4 if heads % 4 == 0 else 2

    def per_head(body):
        def turn(i, carry):
            for u in range(group):
                h = i * group + u
                body(h, pl.ds(pl.multiple_of(h * size, size), size))
            return carry

        lax.fori_loop(0, heads // group, turn, 0)

    def block_states(h, cols):
        along = run_col[h]
        until = jnp.exp(close_row[h][0:1, :] - along)
        since = jnp.exp(along)
        key_high, key_low = split_bf16(k_ref[:, cols].astype(jnp.float32) * until)
        query_high, query_low = split_bf16(q_ref[:, cols].astype(jnp.float32) * since)
        value, grad = v_ref[:, cols], g_ref[:, cols]
        state[0, h] = mm(key_high, value, TN) + mm(key_low, value, TN)
        state[1, h] = mm(query_high, grad, TN) + mm(query_low, grad, TN)

    per_head(block_states)

    def level(index, src, dst, peer):
        return pltpu.make_async_remote_copy(
            src_ref=src,
            dst_ref=dst,
            send_sem=lvl_send.at[index],
            recv_sem=lvl_recv.at[index],
            device_id={"ctx": peer},
            device_id_type=MESH,
        )

    core_state = level(0, state, sib_state, sib)
    core_decay = level(1, own_decay, sib_decay, sib)
    x_state = level(2, chip_state, far_state, xpart)
    x_decay = level(3, chip_decay, far_decay, xpart)
    y_copy = level(4, pair_state.at[ybit], y_state, ypart)
    outer_copy = level(5, outer.at[core], outer.at[core], sib)
    outer_arrival = level(5, outer.at[1 - core], outer.at[1 - core], sib)
    core_state.start()
    core_decay.start()

    def local_parts(h, cols):
        mask = causal_mask(length)
        spread = run_col[h] - run_row[h][0:1, :]
        weights = jnp.where(mask, jnp.exp(jnp.where(mask, spread, 0.0)), 0.0)
        query, key, value, grad = q_ref[:, cols], k_ref[:, cols], v_ref[:, cols], g_ref[:, cols]
        grad_scores = (mm(grad, value, NT) * weights).astype(jnp.bfloat16)
        scores = (mm(query, key, NT) * weights).astype(jnp.bfloat16)
        local[0, :, cols] = mm(grad_scores, key, NN)
        local[1, :, cols] = mm(grad_scores, query, TN)
        local[2, :, cols] = mm(scores, grad, TN)

    core_state.wait_recv()
    core_decay.wait_recv()
    chip_decay[...] = own_decay[...] * sib_decay[...]

    def chip_totals(j, carry):
        h = core * half + j
        mine, theirs = own_decay[h][0:1, :], sib_decay[h][0:1, :]
        s_mine, s_sib = state[0, h], sib_state[0, h]
        g_mine, g_sib = state[1, h], sib_state[1, h]
        first_core = core == 0
        chip_state[0, j] = jnp.where(
            first_core, s_sib + theirs * s_mine, s_mine + mine * s_sib
        ).astype(jnp.bfloat16)
        chip_state[1, j] = jnp.where(
            first_core, g_mine + mine * g_sib, g_sib + theirs * g_mine
        ).astype(jnp.bfloat16)
        return carry

    lax.fori_loop(0, half, chip_totals, 0)
    x_state.start()
    x_decay.start()

    if n_z > 1:
        route_chunk(1)
    per_head(local_parts)

    x_state.wait_recv()
    x_decay.wait_recv()

    def pair_totals(j, carry):
        h = core * half + j
        mine, theirs = chip_decay[h][0:1, :], far_decay[h][0:1, :]
        s_mine, s_far = chip_state[0, j].astype(jnp.float32), far_state[0, j].astype(jnp.float32)
        g_mine, g_far = chip_state[1, j].astype(jnp.float32), far_state[1, j].astype(jnp.float32)
        first_x = xbit == 0
        pair_state[0, j] = jnp.where(
            first_x, s_far + theirs * s_mine, s_mine + mine * s_far
        ).astype(jnp.bfloat16)
        pair_state[1, j] = jnp.where(
            first_x, g_mine + mine * g_far, g_far + theirs * g_mine
        ).astype(jnp.bfloat16)
        return carry

    lax.fori_loop(0, half, pair_totals, 0)
    y_copy.start()

    pass_on(0)
    if n_z > 2:
        route_chunk(2)
    multiply(0)

    y_copy.wait_recv()

    def outer_states(j, carry):
        h = core * half + j
        theirs = far_decay[h][0:1, :]
        from_y = y_state[j].astype(jnp.float32)
        zero = jnp.zeros_like(from_y)
        y_prefix = jnp.where(ybit == 1, from_y, zero)
        y_suffix = jnp.where(ybit == 0, from_y, zero)
        s_far, g_far = far_state[0, j].astype(jnp.float32), far_state[1, j].astype(jnp.float32)
        outer[core, 0, j] = jnp.where(xbit == 1, s_far + theirs * y_prefix, y_prefix)
        outer[core, 1, j] = jnp.where(xbit == 0, g_far + theirs * y_suffix, y_suffix)
        return carry

    lax.fori_loop(0, half, outer_states, 0)
    outer_copy.start()

    if n_z > 1:
        pass_on(1)
    for i in range(3, n_z):
        route_chunk(i)
        multiply(i - 2)
        pass_on(i - 1)

    outer_arrival.wait_recv()

    def finish(h, cols):
        along = run_col[h]
        until = jnp.exp(close_row[h][0:1, :] - along)
        since = jnp.exp(along)
        theirs = sib_decay[h][0:1, :]
        side, j = h // half, h % half
        before, after = outer[side, 0, j], outer[side, 1, j]
        prefix = jnp.where(core == 1, sib_state[0, h] + theirs * before, before)
        suffix = jnp.where(core == 0, sib_state[1, h] + theirs * after, after)
        prefix_high, prefix_low = split_bf16(prefix)
        suffix_high, suffix_low = split_bf16(suffix)
        key, value, grad = k_ref[:, cols], v_ref[:, cols], g_ref[:, cols]
        query_part = mm(grad, prefix_high, NT) + mm(grad, prefix_low, NT)
        key_part = mm(value, suffix_high, NT) + mm(value, suffix_low, NT)
        value_part = mm(key, suffix_high, NN) + mm(key, suffix_low, NN)
        qg_ref[:, cols] = (local[0, :, cols] + since * query_part).astype(jnp.bfloat16)
        kg_ref[:, cols] = (local[1, :, cols] + until * key_part).astype(jnp.bfloat16)
        vg_ref[:, cols] = (local[2, :, cols] + until * value_part).astype(jnp.bfloat16)

    per_head(finish)
    if n_z > 2:
        multiply(n_z - 2)
        pass_on(n_z - 1)
    multiply(n_z - 1)

    @pl.when(has_left)
    def _():
        own_copy(0).wait_send()

    @pl.when(has_right)
    def _():
        own_copy(1).wait_send()

    for i in range(n_z):
        s = chunk_at(i)
        if i:
            to_right, to_left = forwards(s)

            @pl.when(to_right)
            def _():
                forward_copy(i, s, 1).wait_send()

            @pl.when(to_left)
            def _():
                forward_copy(i, s, 0).wait_send()

        for d in range(1, n_chip):
            xy_copy(i, s, d).wait_send()
        for d in range(n_chip):
            sib_copy(s, d).wait_send()
    for copy in (core_state, core_decay, x_state, x_decay, y_copy, outer_copy):
        copy.wait_send()


def fused(
    queries, keys, values, out_grad, log_decay, moe_grad, expert_ids, gate_weights, down_weight
):
    n_ctx, n_z = lax.axis_size("ctx"), lax.axis_size("exp")
    n_chip = n_ctx // 2
    length, heads = log_decay.shape
    width = moe_grad.shape[1]
    size = queries.shape[1] // heads
    cap = 5 * length // (2 * n_chip)
    half = heads // 2
    hidden = down_weight.shape[1]
    bf16, f32 = jnp.bfloat16, jnp.float32
    dma = pltpu.SemaphoreType.DMA
    vmem = pl.BlockSpec(memory_space=pltpu.VMEM)
    decay = pltpu.VMEM((heads, 8, size), f32)
    scratch = [
        pltpu.VMEM((n_z, hidden, width), bf16),
        pltpu.VMEM((n_z, length, width), bf16),
        pltpu.VMEM((n_z, n_chip - 1, cap, width), bf16),
        pltpu.VMEM((n_z, n_ctx, cap, width), bf16),
        pltpu.VMEM((n_chip, 2 * cap, hidden), f32),
        pltpu.VMEM((n_chip, cap, length), bf16),
        pltpu.VMEM((n_chip, cap, 128), f32),
        pltpu.VMEM((heads, length, size), f32),
        pltpu.VMEM((heads, 8, length), f32),
        decay,
        decay,
        decay,
        decay,
        decay,
        pltpu.VMEM((2, heads, size, size), f32),
        pltpu.VMEM((2, heads, size, size), f32),
        pltpu.VMEM((2, half, size, size), bf16),
        pltpu.VMEM((2, half, size, size), bf16),
        pltpu.VMEM((2, half, size, size), bf16),
        pltpu.VMEM((half, size, size), bf16),
        pltpu.VMEM((2, 2, half, size, size), f32),
        pltpu.VMEM((3, length, width), f32),
        dma((n_z,)),
        dma((2,)),
        dma((n_z,)),
        dma((n_z,)),
        dma((n_z, n_chip)),
        dma((n_z, n_chip)),
        dma((n_z, n_chip)),
        dma((n_z, n_chip)),
        dma((6,)),
        dma((6,)),
    ]
    flat = jax.ShapeDtypeStruct((length, heads * size), bf16)
    return pl.pallas_call(
        functools.partial(fused_kernel, (n_z, n_chip, cap, heads, size)),
        out_shape=(
            flat,
            flat,
            flat,
            jax.ShapeDtypeStruct((1, n_ctx * cap, hidden), bf16),
        ),
        in_specs=[vmem] * 8 + [pl.BlockSpec(memory_space=pl.ANY)],
        out_specs=(vmem,) * 4,
        scratch_shapes=scratch,
        compiler_params=pltpu.CompilerParams(
            collective_id=0, has_side_effects=True, vmem_limit_bytes=52 * 2**20
        ),
    )(queries, keys, values, out_grad, log_decay, moe_grad, expert_ids, gate_weights, down_weight)


def body(
    queries, keys, values, out_grad, log_decay, moe_grad, expert_ids, gate_weights, down_weight
):
    n_ctx, n_z = lax.axis_size("ctx"), lax.axis_size("exp")
    length, heads = log_decay.shape
    cap = 5 * length // n_ctx
    args = (
        queries, keys, values, out_grad, log_decay, moe_grad, expert_ids, gate_weights, down_weight
    )
    size = queries.shape[1] // heads
    fits = (
        n_ctx == 8
        and n_z > 2
        and cap % 16 == 0
        and size == 128
        and length == 128
        and heads % 2 == 0
        and moe_grad.shape[1] % 128 == 0
        and queries.shape[1] == moe_grad.shape[1]
    )
    return fused(*args) if fits else per_device(*args)


def solution(mesh):
    in_specs = (
        P("ctx", "exp"),
        P("ctx", "exp"),
        P("ctx", "exp"),
        P("ctx", "exp"),
        P("ctx", "exp"),
        P("ctx", "exp"),
        P("ctx", None),
        P("ctx", None),
        P("ctx", "exp", None),
    )
    out_specs = (P("ctx", "exp"), P("ctx", "exp"), P("ctx", "exp"), P("ctx", None, "exp"))
    return jax.shard_map(
        body, mesh=mesh, in_specs=in_specs, out_specs=out_specs, check_vma=False
    )
```

```python
import functools

import jax
import jax.numpy as jnp
from jax import lax
from jax.experimental import pallas as pl
from jax.experimental.pallas import tpu as pltpu
from jax.sharding import PartitionSpec as P


def carried_in(x, axis, combine, identity, reverse):
    devices, place = (lax.axis_size(axis), lax.axis_index(axis))
    everything = jax.tree.map(lambda part: lax.all_gather(part, axis), x)
    start = jax.tree.map(
        lambda part, zero: jnp.broadcast_to(jnp.asarray(zero, part.dtype), part.shape), x, identity
    )

    def turn(k, before):
        at = devices - 1 - k if reverse else k
        reached = at > place if reverse else at < place
        new = combine(before, jax.tree.map(lambda part: part[at], everything))
        return jax.tree.map(lambda a, b: jnp.where(reached, a, b), new, before)

    return lax.fori_loop(0, devices, turn, start)


def partner_2(value, axis, apart):
    mask = 2**apart
    pairs = [(source, source ^ mask) for source in range(lax.axis_size(axis))]
    return lax.ppermute(value, axis, pairs)


def combine_states(earlier, later):
    return (later[1][:, None, None] * earlier[0] + later[0], earlier[1] * later[1])


def attention_grads(queries, keys, values, out_grad, log_decay):
    length, head_count = log_decay.shape
    head_size = queries.shape[1] // head_count
    query_h = queries.reshape(length, head_count, head_size)
    key_h = keys.reshape(length, head_count, head_size)
    value_h = values.reshape(length, head_count, head_size)
    grad_h = out_grad.reshape(length, head_count, head_size)
    running = jnp.cumsum(log_decay, axis=0)
    closing = running[-1]
    causal = jnp.arange(length)[:, None] >= jnp.arange(length)[None, :]
    spread = running.T[:, :, None] - running.T[:, None, :]
    weights = jnp.where(causal[None], jnp.exp(jnp.where(causal[None], spread, 0.0)), 0.0)
    until_finish = jnp.exp(closing[None, :] - running)
    since_beginning = jnp.exp(running)
    query_full = query_h.astype(jnp.float32)
    key_full = key_h.astype(jnp.float32)
    value_full = value_h.astype(jnp.float32)
    gradient_full = grad_h.astype(jnp.float32)
    block_state = jnp.einsum(
        "jqz,jqb->qzb",
        key_full * until_finish[:, :, None],
        value_full,
        precision=lax.Precision.HIGHEST,
    )
    block_grad = jnp.einsum(
        "soj,sop->ojp",
        query_full * since_beginning[:, :, None],
        gradient_full,
        precision=lax.Precision.HIGHEST,
    )
    block_decay = jnp.exp(closing)
    identity_pair = (jnp.zeros_like(block_state), jnp.ones_like(block_decay))
    leading_part, _ = carried_in(
        (block_state, block_decay), "ctx", combine_states, identity_pair, False
    )
    trailing_part, _ = carried_in(
        (block_grad, block_decay), "ctx", combine_states, identity_pair, True
    )
    grad_scores = (
        jnp.einsum("thv,shv->hts", grad_h, value_h, preferred_element_type=jnp.float32) * weights
    ).astype(jnp.bfloat16)
    scores = (
        jnp.einsum("thk,shk->hts", query_h, key_h, preferred_element_type=jnp.float32) * weights
    ).astype(jnp.bfloat16)
    query_grad = jnp.einsum(
        "hts,shk->thk", grad_scores, key_h, preferred_element_type=jnp.float32
    ) + since_beginning[:, :, None] * jnp.einsum(
        "xrq,rgq->xrg", gradient_full, leading_part, precision=lax.Precision.HIGHEST
    )
    key_grad = jnp.einsum(
        "hts,thk->shk", grad_scores, query_h, preferred_element_type=jnp.float32
    ) + until_finish[:, :, None] * jnp.einsum(
        "pox,ofx->pof", value_full, trailing_part, precision=lax.Precision.HIGHEST
    )
    value_grad = jnp.einsum(
        "hts,thv->shv", scores, grad_h, preferred_element_type=jnp.float32
    ) + until_finish[:, :, None] * jnp.einsum(
        "raj,ajb->rab", key_full, trailing_part, precision=lax.Precision.HIGHEST
    )
    flat_width = head_count * head_size
    return (
        query_grad.reshape(length, flat_width).astype(jnp.bfloat16),
        key_grad.reshape(length, flat_width).astype(jnp.bfloat16),
        value_grad.reshape(length, flat_width).astype(jnp.bfloat16),
    )


def route_rows(moe_grad, expert_ids, gate_weights, experts, capacity):
    pair_ids = expert_ids.reshape(-1)
    onehot = (pair_ids[:, None] == jnp.arange(experts)[None, :]).astype(jnp.int32)
    earlier = jnp.cumsum(onehot, axis=0) - onehot
    pair_slots = (pair_ids * capacity + jnp.sum(earlier * onehot, axis=1)).reshape(-1, 2)
    slot_iota = jnp.arange(experts * capacity)[:, None]
    first_table = jnp.where(
        slot_iota == pair_slots[:, 0][None, :], gate_weights[:, 0][None, :], 0.0
    )
    second_table = jnp.where(
        slot_iota == pair_slots[:, 1][None, :], gate_weights[:, 1][None, :], 0.0
    )
    dispatch_table = first_table + second_table
    return jnp.dot(
        dispatch_table, moe_grad.astype(jnp.float32), precision=lax.Precision.HIGHEST
    ).astype(jnp.bfloat16)


def per_device(
    queries, keys, values, out_grad, log_decay, moe_grad, expert_ids, gate_weights, down_weight
):
    query_grad, key_grad, value_grad = attention_grads(queries, keys, values, out_grad, log_decay)
    devices_ctx = lax.axis_size("ctx")
    experts = devices_ctx // 2
    length = moe_grad.shape[0]
    capacity = 5 * length // (2 * experts)
    routed = route_rows(moe_grad, expert_ids, gate_weights, experts, capacity)
    weight_slab = down_weight[0]
    half_count = capacity // 2
    own_rows = lax.all_to_all(routed, "ctx", split_axis=0, concat_axis=0, tiled=True)
    own_full = lax.all_gather(own_rows, "exp", axis=1, tiled=True)
    partner = partner_2(own_full, "ctx", 0)
    parity = lax.axis_index("ctx") % 2
    own_view = own_full.reshape(devices_ctx, half_count, -1)
    partner_view = partner.reshape(devices_ctx, half_count, -1)
    lower_half = jnp.where(parity == 0, own_view, partner_view)
    upper_half = jnp.where(parity == 0, partner_view, own_view)
    all_rows = jnp.concatenate([lower_half, upper_half], axis=1).reshape(devices_ctx * capacity, -1)
    hidden = jnp.einsum("sd,fd->sf", all_rows, weight_slab, preferred_element_type=jnp.float32)
    hidden_grad = hidden.astype(jnp.bfloat16)[None]
    return (query_grad, key_grad, value_grad, hidden_grad)


MESH = pl.DeviceIdType.MESH
NT = (((1,), (1,)), ((), ()))
NN = (((1,), (0,)), ((), ()))
TN = (((0,), (0,)), ((), ()))


def mm(a, b, dims, precision=None):
    return lax.dot_general(a, b, dims, precision=precision, preferred_element_type=jnp.float32)


def split_bf16(x):
    high = x.astype(jnp.bfloat16)
    return high, (x - high.astype(jnp.float32)).astype(jnp.bfloat16)


def causal_mask(size):
    return lax.broadcasted_iota(jnp.int32, (size, size), 0) >= lax.broadcasted_iota(
        jnp.int32, (size, size), 1
    )


def fused_kernel(
    sizes,
    q_ref,
    k_ref,
    v_ref,
    g_ref,
    ld_ref,
    moe_ref,
    ids_ref,
    gate_ref,
    w_hbm,
    qg_ref,
    kg_ref,
    vg_ref,
    hid_ref,
    wbuf,
    raw,
    sendbuf,
    rows,
    acc,
    table,
    slot_gate,
    run_col,
    run_row,
    close_row,
    own_decay,
    sib_decay,
    chip_decay,
    far_decay,
    state,
    sib_state,
    chip_state,
    far_state,
    pair_state,
    y_state,
    outer,
    local,
    w_sem,
    own_send,
    relay_send,
    fwd_send,
    raw_recv,
    xy_send,
    xy_recv,
    zp_send,
    zp_recv,
    sib_send,
    sib_recv,
    lvl_send,
    lvl_recv,
):
    n_z, n_chip, cap, heads, size = sizes
    half = heads // 2
    length = moe_ref.shape[0]
    width = moe_ref.shape[1]
    c, z = lax.axis_index("ctx"), lax.axis_index("exp")
    core = c % 2
    chip = c // 2
    xbit, ybit = chip % 2, chip // 2
    sib = c + 1 - 2 * core
    xpart = c + 2 - 4 * xbit
    ypart = c + 4 - 8 * ybit
    upper_half, odd = z // 2, z % 2
    partner = z + 1 - 2 * odd
    across = n_z - 1 - z
    inner = odd + upper_half - 2 * odd * upper_half
    toward = z + 1 - 2 * upper_half

    def chip_at(d):
        return (chip + d) % n_chip

    barrier = pltpu.get_barrier_semaphore()
    for d in range(1, n_chip):
        pl.semaphore_signal(
            barrier, inc=1, device_id={"ctx": chip_at(d) * 2 + core}, device_id_type=MESH
        )
    pl.semaphore_signal(barrier, inc=1, device_id={"ctx": sib}, device_id_type=MESH)

    pl.semaphore_signal(barrier, inc=1, device_id={"exp": partner}, device_id_type=MESH)

    @pl.when(inner == 1)
    def _():
        pl.semaphore_signal(barrier, inc=1, device_id={"exp": across}, device_id_type=MESH)

    pl.semaphore_wait(barrier, n_chip + 1 + inner)

    def raw_copy(src, s, send_sem, to):
        return pltpu.make_async_remote_copy(
            src_ref=src,
            dst_ref=raw.at[s],
            send_sem=send_sem,
            recv_sem=raw_recv.at[s],
            device_id={"exp": to},
            device_id_type=MESH,
        )

    own_copy = raw_copy(moe_ref, z, own_send, toward)
    own_copy.start()
    relay_copy = raw_copy(raw.at[partner], partner, relay_send, across)

    w_copies = [
        pltpu.make_async_copy(w_hbm.at[0, :, pl.ds(i * width, width)], wbuf.at[i], w_sem.at[i])
        for i in range(n_z)
    ]
    for copy in w_copies:
        copy.start()

    def chunk_at(i):
        return 1 + i + upper_half * (1 - 2 * i) if i else z

    def forward_copy(i):
        s = chunk_at(i)
        return raw_copy(raw.at[s], s, fwd_send.at[i], partner)

    ids = ids_ref[...]
    gates = gate_ref[...]
    expert = lax.broadcasted_iota(jnp.int32, (8, length), 0)
    first, second = ids[0:1, :] == expert, ids[1:2, :] == expert
    named_row = (first | second).astype(jnp.float32)
    weight_row = jnp.where(first, gates[0:1, :], 0.0) + jnp.where(second, gates[1:2, :], 0.0)
    t_row = lax.broadcasted_iota(jnp.int32, (length, length), 0)
    t_col = lax.broadcasted_iota(jnp.int32, (length, length), 1)
    earlier = (t_row < t_col).astype(jnp.float32)
    rank_row = mm(named_row, earlier, NN)
    slot = lax.broadcasted_iota(jnp.int32, (cap, length), 0).astype(jnp.float32)
    for e in range(n_chip):
        hit = (rank_row[e : e + 1, :] == slot) & (named_row[e : e + 1, :] > 0.5)
        table[e] = hit.astype(jnp.float32).astype(jnp.bfloat16)
        gate = jnp.sum(jnp.where(hit, weight_row[e : e + 1, :], 0.0), axis=1, keepdims=True)
        slot_gate[e] = jnp.broadcast_to(gate, (cap, 128))

    def xy_copy(i, s, d):
        return pltpu.make_async_remote_copy(
            src_ref=sendbuf.at[i, d - 1],
            dst_ref=rows.at[s, c],
            send_sem=xy_send.at[i, d],
            recv_sem=xy_recv.at[s, chip],
            device_id={"ctx": chip_at(d) * 2 + core},
            device_id_type=MESH,
        )

    def xy_arrival(i, s, d):
        source = chip_at(d)
        return pltpu.make_async_remote_copy(
            src_ref=sendbuf.at[i, d - 1],
            dst_ref=rows.at[s, source * 2 + core],
            send_sem=xy_send.at[i, d],
            recv_sem=xy_recv.at[s, source],
            device_id={"ctx": source * 2 + core},
            device_id_type=MESH,
        )

    def sib_copy(s, d):
        block = rows.at[s, chip_at(d) * 2 + core]
        return pltpu.make_async_remote_copy(
            src_ref=block,
            dst_ref=block,
            send_sem=sib_send.at[s, d],
            recv_sem=sib_recv.at[s, d],
            device_id={"ctx": sib},
            device_id_type=MESH,
        )

    def sib_arrival(s, d):
        block = rows.at[s, chip_at(d) * 2 + 1 - core]
        return pltpu.make_async_remote_copy(
            src_ref=block,
            dst_ref=block,
            send_sem=sib_send.at[s, d],
            recv_sem=sib_recv.at[s, d],
            device_id={"ctx": sib},
            device_id_type=MESH,
        )

    def zp_copy(s, d):
        block = rows.at[s, chip_at(d) * 2 + core]
        return pltpu.make_async_remote_copy(
            src_ref=block,
            dst_ref=block,
            send_sem=zp_send.at[d],
            recv_sem=zp_recv.at[d],
            device_id={"exp": partner},
            device_id_type=MESH,
        )

    def take(i):
        forward_copy(i).wait_recv()

        @pl.when(inner == 1)
        def _():
            forward_copy(i).start()

    def route_chunk(i):
        s = chunk_at(i)
        for d in (*range(1, n_chip), 0):
            e = chip_at(d)
            picked = mm(table[e], raw[s] if i else moe_ref[...], NN)
            routed = (picked * slot_gate[e][:, 0:1]).astype(jnp.bfloat16)
            if d:
                sendbuf[i, d - 1] = routed
                xy_copy(i, s, d).start()
            else:
                rows[s, c] = routed
                sib_copy(s, 0).start()

    def pass_on(i):
        s = chunk_at(i)
        for d in range(1, n_chip):
            xy_arrival(i, s, d).wait_recv()
            sib_copy(s, d).start()

    def multiply(s, first=False, last=False):
        if first:
            for copy in w_copies:
                copy.wait()

        def tile(j):
            left = rows[s, pl.ds(2 * j, 2)].reshape(2 * cap, width)
            part = mm(left, wbuf[s], NT)
            if not first:
                part = part + acc[j]
            if last:
                hid_ref[0, pl.ds(pl.multiple_of(j * 2 * cap, 2 * cap), 2 * cap), :] = part.astype(
                    jnp.bfloat16
                )
            else:
                acc[j] = part

        for d in range(n_chip):
            sib_arrival(s, d).wait_recv()
            tile(chip_at(d))

    route_chunk(0)

    log_decay = ld_ref[...]
    highest = lax.Precision.HIGHEST
    lower = (t_row >= t_col).astype(jnp.float32)
    upper = (t_row <= t_col).astype(jnp.float32)
    running = mm(lower, log_decay, NT, highest)
    running_t = mm(log_decay, upper, NN, highest)
    closing = mm(log_decay, jnp.ones((length, size), jnp.float32), NN, highest)
    for h in range(heads):
        run_col[h] = jnp.broadcast_to(running[:, h : h + 1], (length, size))
        run_row[h] = jnp.broadcast_to(running_t[h : h + 1, :], (8, length))
        close_row[h] = jnp.broadcast_to(closing[h : h + 1, :], (8, size))
        own_decay[h] = jnp.broadcast_to(jnp.exp(closing[h : h + 1, :]), (8, size))

    group = 4 if heads % 4 == 0 else 2

    def per_head(body):
        def turn(i, carry):
            for u in range(group):
                h = i * group + u
                body(h, pl.ds(pl.multiple_of(h * size, size), size))
            return carry

        lax.fori_loop(0, heads // group, turn, 0)

    def block_states(h, cols):
        along = run_col[h]
        until = jnp.exp(close_row[h][0:1, :] - along)
        since = jnp.exp(along)
        key_high, key_low = split_bf16(k_ref[:, cols].astype(jnp.float32) * until)
        query_high, query_low = split_bf16(q_ref[:, cols].astype(jnp.float32) * since)
        value, grad = v_ref[:, cols], g_ref[:, cols]
        state[0, h] = mm(key_high, value, TN) + mm(key_low, value, TN)
        state[1, h] = mm(query_high, grad, TN) + mm(query_low, grad, TN)

    per_head(block_states)

    def level(index, src, dst, peer):
        return pltpu.make_async_remote_copy(
            src_ref=src,
            dst_ref=dst,
            send_sem=lvl_send.at[index],
            recv_sem=lvl_recv.at[index],
            device_id={"ctx": peer},
            device_id_type=MESH,
        )

    core_state = level(0, state, sib_state, sib)
    core_decay = level(1, own_decay, sib_decay, sib)
    x_state = level(2, chip_state, far_state, xpart)
    x_decay = level(3, chip_decay, far_decay, xpart)
    y_copy = level(4, pair_state.at[ybit], y_state, ypart)
    outer_copy = level(5, outer.at[core], outer.at[core], sib)
    outer_arrival = level(5, outer.at[1 - core], outer.at[1 - core], sib)
    core_state.start()
    core_decay.start()

    def local_parts(h, cols):
        mask = causal_mask(length)
        spread = run_col[h] - run_row[h][0:1, :]
        weights = jnp.where(mask, jnp.exp(jnp.where(mask, spread, 0.0)), 0.0)
        query, key, value, grad = q_ref[:, cols], k_ref[:, cols], v_ref[:, cols], g_ref[:, cols]
        grad_scores = (mm(grad, value, NT) * weights).astype(jnp.bfloat16)
        scores = (mm(query, key, NT) * weights).astype(jnp.bfloat16)
        local[0, :, cols] = mm(grad_scores, key, NN)
        local[1, :, cols] = mm(grad_scores, query, TN)
        local[2, :, cols] = mm(scores, grad, TN)

    @pl.when(inner == 1)
    def _():
        relay_copy.wait_recv()
        relay_copy.start()

    take(1)

    core_state.wait_recv()
    core_decay.wait_recv()
    chip_decay[...] = own_decay[...] * sib_decay[...]

    def chip_totals(j, carry):
        h = core * half + j
        mine, theirs = own_decay[h][0:1, :], sib_decay[h][0:1, :]
        s_mine, s_sib = state[0, h], sib_state[0, h]
        g_mine, g_sib = state[1, h], sib_state[1, h]
        first_core = core == 0
        chip_state[0, j] = jnp.where(
            first_core, s_sib + theirs * s_mine, s_mine + mine * s_sib
        ).astype(jnp.bfloat16)
        chip_state[1, j] = jnp.where(
            first_core, g_mine + mine * g_sib, g_sib + theirs * g_mine
        ).astype(jnp.bfloat16)
        return carry

    lax.fori_loop(0, half, chip_totals, 0)
    x_state.start()
    x_decay.start()

    route_chunk(1)
    pass_on(0)
    per_head(local_parts)
    take(2)
    for d in range(n_chip):
        zp_copy(z, d).start()
    multiply(z, first=True)

    x_state.wait_recv()
    x_decay.wait_recv()

    def pair_totals(j, carry):
        h = core * half + j
        mine, theirs = chip_decay[h][0:1, :], far_decay[h][0:1, :]
        s_mine, s_far = chip_state[0, j].astype(jnp.float32), far_state[0, j].astype(jnp.float32)
        g_mine, g_far = chip_state[1, j].astype(jnp.float32), far_state[1, j].astype(jnp.float32)
        first_x = xbit == 0
        pair_state[0, j] = jnp.where(
            first_x, s_far + theirs * s_mine, s_mine + mine * s_far
        ).astype(jnp.bfloat16)
        pair_state[1, j] = jnp.where(
            first_x, g_mine + mine * g_far, g_far + theirs * g_mine
        ).astype(jnp.bfloat16)
        return carry

    lax.fori_loop(0, half, pair_totals, 0)
    y_copy.start()

    route_chunk(2)

    y_copy.wait_recv()

    def outer_states(j, carry):
        h = core * half + j
        theirs = far_decay[h][0:1, :]
        from_y = y_state[j].astype(jnp.float32)
        zero = jnp.zeros_like(from_y)
        y_prefix = jnp.where(ybit == 1, from_y, zero)
        y_suffix = jnp.where(ybit == 0, from_y, zero)
        s_far, g_far = far_state[0, j].astype(jnp.float32), far_state[1, j].astype(jnp.float32)
        outer[core, 0, j] = jnp.where(xbit == 1, s_far + theirs * y_prefix, y_prefix)
        outer[core, 1, j] = jnp.where(xbit == 0, g_far + theirs * y_suffix, y_suffix)
        return carry

    lax.fori_loop(0, half, outer_states, 0)
    outer_copy.start()

    pass_on(1)
    multiply(chunk_at(1))

    outer_arrival.wait_recv()

    def finish(h, cols):
        along = run_col[h]
        until = jnp.exp(close_row[h][0:1, :] - along)
        since = jnp.exp(along)
        theirs = sib_decay[h][0:1, :]
        side, j = h // half, h % half
        before, after = outer[side, 0, j], outer[side, 1, j]
        prefix = jnp.where(core == 1, sib_state[0, h] + theirs * before, before)
        suffix = jnp.where(core == 0, sib_state[1, h] + theirs * after, after)
        prefix_high, prefix_low = split_bf16(prefix)
        suffix_high, suffix_low = split_bf16(suffix)
        key, value, grad = k_ref[:, cols], v_ref[:, cols], g_ref[:, cols]
        query_part = mm(grad, prefix_high, NT) + mm(grad, prefix_low, NT)
        key_part = mm(value, suffix_high, NT) + mm(value, suffix_low, NT)
        value_part = mm(key, suffix_high, NN) + mm(key, suffix_low, NN)
        qg_ref[:, cols] = (local[0, :, cols] + since * query_part).astype(jnp.bfloat16)
        kg_ref[:, cols] = (local[1, :, cols] + until * key_part).astype(jnp.bfloat16)
        vg_ref[:, cols] = (local[2, :, cols] + until * value_part).astype(jnp.bfloat16)

    per_head(finish)
    pass_on(2)
    multiply(chunk_at(2))
    for d in range(n_chip):
        zp_copy(partner, d).wait_recv()
        sib_copy(partner, d).start()
    multiply(partner, last=True)

    own_copy.wait_send()

    @pl.when(inner == 1)
    def _():
        relay_copy.wait_send()
        for i in range(1, n_z - 1):
            forward_copy(i).wait_send()

    for i in range(n_z - 1):
        s = chunk_at(i)
        for d in range(1, n_chip):
            xy_copy(i, s, d).wait_send()
        for d in range(n_chip):
            sib_copy(s, d).wait_send()
    for d in range(n_chip):
        zp_copy(z, d).wait_send()
        sib_copy(partner, d).wait_send()
    for copy in (core_state, core_decay, x_state, x_decay, y_copy, outer_copy):
        copy.wait_send()


def fused(
    queries, keys, values, out_grad, log_decay, moe_grad, expert_ids, gate_weights, down_weight
):
    n_ctx, n_z = lax.axis_size("ctx"), lax.axis_size("exp")
    n_chip = n_ctx // 2
    length, heads = log_decay.shape
    width = moe_grad.shape[1]
    size = queries.shape[1] // heads
    cap = 5 * length // (2 * n_chip)
    half = heads // 2
    hidden = down_weight.shape[1]
    bf16, f32 = jnp.bfloat16, jnp.float32
    dma = pltpu.SemaphoreType.DMA
    vmem = pl.BlockSpec(memory_space=pltpu.VMEM)
    decay = pltpu.VMEM((heads, 8, size), f32)
    scratch = [
        pltpu.VMEM((n_z, hidden, width), bf16),
        pltpu.VMEM((n_z, length, width), bf16),
        pltpu.VMEM((n_z - 1, n_chip - 1, cap, width), bf16),
        pltpu.VMEM((n_z, n_ctx, cap, width), bf16),
        pltpu.VMEM((n_chip, 2 * cap, hidden), f32),
        pltpu.VMEM((n_chip, cap, length), bf16),
        pltpu.VMEM((n_chip, cap, 128), f32),
        pltpu.VMEM((heads, length, size), f32),
        pltpu.VMEM((heads, 8, length), f32),
        decay,
        decay,
        decay,
        decay,
        decay,
        pltpu.VMEM((2, heads, size, size), f32),
        pltpu.VMEM((2, heads, size, size), f32),
        pltpu.VMEM((2, half, size, size), bf16),
        pltpu.VMEM((2, half, size, size), bf16),
        pltpu.VMEM((2, half, size, size), bf16),
        pltpu.VMEM((half, size, size), bf16),
        pltpu.VMEM((2, 2, half, size, size), f32),
        pltpu.VMEM((3, length, width), f32),
        dma((n_z,)),
        dma,
        dma,
        dma((n_z - 1,)),
        dma((n_z,)),
        dma((n_z - 1, n_chip)),
        dma((n_z, n_chip)),
        dma((n_chip,)),
        dma((n_chip,)),
        dma((n_z, n_chip)),
        dma((n_z, n_chip)),
        dma((6,)),
        dma((6,)),
    ]
    flat = jax.ShapeDtypeStruct((length, heads * size), bf16)
    return pl.pallas_call(
        functools.partial(fused_kernel, (n_z, n_chip, cap, heads, size)),
        out_shape=(
            flat,
            flat,
            flat,
            jax.ShapeDtypeStruct((1, n_ctx * cap, hidden), bf16),
        ),
        in_specs=[vmem] * 8 + [pl.BlockSpec(memory_space=pl.ANY)],
        out_specs=(vmem,) * 4,
        scratch_shapes=scratch,
        compiler_params=pltpu.CompilerParams(
            collective_id=0, has_side_effects=True, vmem_limit_bytes=52 * 2**20
        ),
    )(
        queries,
        keys,
        values,
        out_grad,
        log_decay.T,
        moe_grad,
        expert_ids.T,
        gate_weights.T,
        down_weight,
    )


def body(
    queries, keys, values, out_grad, log_decay, moe_grad, expert_ids, gate_weights, down_weight
):
    n_ctx, n_z = lax.axis_size("ctx"), lax.axis_size("exp")
    length, heads = log_decay.shape
    cap = 5 * length // n_ctx
    args = (
        queries, keys, values, out_grad, log_decay, moe_grad, expert_ids, gate_weights, down_weight
    )
    size = queries.shape[1] // heads
    fits = (
        n_ctx == 8
        and n_z == 4
        and cap % 16 == 0
        and size == 128
        and length == 128
        and heads % 2 == 0
        and moe_grad.shape[1] % 128 == 0
        and queries.shape[1] == moe_grad.shape[1]
    )
    return fused(*args) if fits else per_device(*args)


def solution(mesh):
    in_specs = (
        P("ctx", "exp"),
        P("ctx", "exp"),
        P("ctx", "exp"),
        P("ctx", "exp"),
        P("ctx", "exp"),
        P("ctx", "exp"),
        P("ctx", None),
        P("ctx", None),
        P("ctx", "exp", None),
    )
    out_specs = (P("ctx", "exp"), P("ctx", "exp"), P("ctx", "exp"), P("ctx", None, "exp"))
    return jax.shard_map(
        body, mesh=mesh, in_specs=in_specs, out_specs=out_specs, check_vma=False
    )
```

```python
import functools

import jax
import jax.numpy as jnp
from jax import lax
from jax.experimental import pallas as pl
from jax.experimental.pallas import tpu as pltpu
from jax.sharding import PartitionSpec as P


def carried_in(x, axis, combine, identity, reverse):
    devices, place = (lax.axis_size(axis), lax.axis_index(axis))
    everything = jax.tree.map(lambda part: lax.all_gather(part, axis), x)
    start = jax.tree.map(
        lambda part, zero: jnp.broadcast_to(jnp.asarray(zero, part.dtype), part.shape), x, identity
    )

    def turn(k, before):
        at = devices - 1 - k if reverse else k
        reached = at > place if reverse else at < place
        new = combine(before, jax.tree.map(lambda part: part[at], everything))
        return jax.tree.map(lambda a, b: jnp.where(reached, a, b), new, before)

    return lax.fori_loop(0, devices, turn, start)


def partner_2(value, axis, apart):
    mask = 2**apart
    pairs = [(source, source ^ mask) for source in range(lax.axis_size(axis))]
    return lax.ppermute(value, axis, pairs)


def combine_states(earlier, later):
    return (later[1][:, None, None] * earlier[0] + later[0], earlier[1] * later[1])


def attention_grads(queries, keys, values, out_grad, log_decay):
    length, head_count = log_decay.shape
    head_size = queries.shape[1] // head_count
    query_h = queries.reshape(length, head_count, head_size)
    key_h = keys.reshape(length, head_count, head_size)
    value_h = values.reshape(length, head_count, head_size)
    grad_h = out_grad.reshape(length, head_count, head_size)
    running = jnp.cumsum(log_decay, axis=0)
    closing = running[-1]
    causal = jnp.arange(length)[:, None] >= jnp.arange(length)[None, :]
    spread = running.T[:, :, None] - running.T[:, None, :]
    weights = jnp.where(causal[None], jnp.exp(jnp.where(causal[None], spread, 0.0)), 0.0)
    until_finish = jnp.exp(closing[None, :] - running)
    since_beginning = jnp.exp(running)
    query_full = query_h.astype(jnp.float32)
    key_full = key_h.astype(jnp.float32)
    value_full = value_h.astype(jnp.float32)
    gradient_full = grad_h.astype(jnp.float32)
    block_state = jnp.einsum(
        "jqz,jqb->qzb",
        key_full * until_finish[:, :, None],
        value_full,
        precision=lax.Precision.HIGHEST,
    )
    block_grad = jnp.einsum(
        "soj,sop->ojp",
        query_full * since_beginning[:, :, None],
        gradient_full,
        precision=lax.Precision.HIGHEST,
    )
    block_decay = jnp.exp(closing)
    identity_pair = (jnp.zeros_like(block_state), jnp.ones_like(block_decay))
    leading_part, _ = carried_in(
        (block_state, block_decay), "ctx", combine_states, identity_pair, False
    )
    trailing_part, _ = carried_in(
        (block_grad, block_decay), "ctx", combine_states, identity_pair, True
    )
    grad_scores = (
        jnp.einsum("thv,shv->hts", grad_h, value_h, preferred_element_type=jnp.float32) * weights
    ).astype(jnp.bfloat16)
    scores = (
        jnp.einsum("thk,shk->hts", query_h, key_h, preferred_element_type=jnp.float32) * weights
    ).astype(jnp.bfloat16)
    query_grad = jnp.einsum(
        "hts,shk->thk", grad_scores, key_h, preferred_element_type=jnp.float32
    ) + since_beginning[:, :, None] * jnp.einsum(
        "xrq,rgq->xrg", gradient_full, leading_part, precision=lax.Precision.HIGHEST
    )
    key_grad = jnp.einsum(
        "hts,thk->shk", grad_scores, query_h, preferred_element_type=jnp.float32
    ) + until_finish[:, :, None] * jnp.einsum(
        "pox,ofx->pof", value_full, trailing_part, precision=lax.Precision.HIGHEST
    )
    value_grad = jnp.einsum(
        "hts,thv->shv", scores, grad_h, preferred_element_type=jnp.float32
    ) + until_finish[:, :, None] * jnp.einsum(
        "raj,ajb->rab", key_full, trailing_part, precision=lax.Precision.HIGHEST
    )
    flat_width = head_count * head_size
    return (
        query_grad.reshape(length, flat_width).astype(jnp.bfloat16),
        key_grad.reshape(length, flat_width).astype(jnp.bfloat16),
        value_grad.reshape(length, flat_width).astype(jnp.bfloat16),
    )


def route_rows(moe_grad, expert_ids, gate_weights, experts, capacity):
    pair_ids = expert_ids.reshape(-1)
    onehot = (pair_ids[:, None] == jnp.arange(experts)[None, :]).astype(jnp.int32)
    earlier = jnp.cumsum(onehot, axis=0) - onehot
    pair_slots = (pair_ids * capacity + jnp.sum(earlier * onehot, axis=1)).reshape(-1, 2)
    slot_iota = jnp.arange(experts * capacity)[:, None]
    first_table = jnp.where(
        slot_iota == pair_slots[:, 0][None, :], gate_weights[:, 0][None, :], 0.0
    )
    second_table = jnp.where(
        slot_iota == pair_slots[:, 1][None, :], gate_weights[:, 1][None, :], 0.0
    )
    dispatch_table = first_table + second_table
    return jnp.dot(
        dispatch_table, moe_grad.astype(jnp.float32), precision=lax.Precision.HIGHEST
    ).astype(jnp.bfloat16)


def per_device(
    queries, keys, values, out_grad, log_decay, moe_grad, expert_ids, gate_weights, down_weight
):
    query_grad, key_grad, value_grad = attention_grads(queries, keys, values, out_grad, log_decay)
    devices_ctx = lax.axis_size("ctx")
    experts = devices_ctx // 2
    length = moe_grad.shape[0]
    capacity = 5 * length // (2 * experts)
    routed = route_rows(moe_grad, expert_ids, gate_weights, experts, capacity)
    weight_slab = down_weight[0]
    half_count = capacity // 2
    own_rows = lax.all_to_all(routed, "ctx", split_axis=0, concat_axis=0, tiled=True)
    own_full = lax.all_gather(own_rows, "exp", axis=1, tiled=True)
    partner = partner_2(own_full, "ctx", 0)
    parity = lax.axis_index("ctx") % 2
    own_view = own_full.reshape(devices_ctx, half_count, -1)
    partner_view = partner.reshape(devices_ctx, half_count, -1)
    lower_half = jnp.where(parity == 0, own_view, partner_view)
    upper_half = jnp.where(parity == 0, partner_view, own_view)
    all_rows = jnp.concatenate([lower_half, upper_half], axis=1).reshape(devices_ctx * capacity, -1)
    hidden = jnp.einsum("sd,fd->sf", all_rows, weight_slab, preferred_element_type=jnp.float32)
    hidden_grad = hidden.astype(jnp.bfloat16)[None]
    return (query_grad, key_grad, value_grad, hidden_grad)


MESH = pl.DeviceIdType.MESH
NT = (((1,), (1,)), ((), ()))
NN = (((1,), (0,)), ((), ()))
TN = (((0,), (0,)), ((), ()))


def mm(a, b, dims, precision=None):
    return lax.dot_general(a, b, dims, precision=precision, preferred_element_type=jnp.float32)


def split_bf16(x):
    high = x.astype(jnp.bfloat16)
    return high, (x - high.astype(jnp.float32)).astype(jnp.bfloat16)


def causal_mask(size):
    return lax.broadcasted_iota(jnp.int32, (size, size), 0) >= lax.broadcasted_iota(
        jnp.int32, (size, size), 1
    )


def fused_kernel(
    sizes,
    q_hbm,
    k_hbm,
    v_hbm,
    g_hbm,
    ld_ref,
    moe_ref,
    ids_ref,
    gate_ref,
    w_hbm,
    qg_hbm,
    kg_hbm,
    vg_hbm,
    hid_hbm,
    q_ref,
    k_ref,
    v_ref,
    g_ref,
    grads,
    hid,
    wbuf,
    raw,
    sendbuf,
    rows,
    acc,
    table,
    near_table,
    slot_gate,
    run_col,
    run_row,
    close_row,
    own_decay,
    sib_decay,
    chip_decay,
    far_decay,
    state,
    sib_state,
    chip_state,
    far_state,
    pair_state,
    y_state,
    outer,
    local,
    in_sem,
    out_sem,
    hid_sem,
    moe_sem,
    w_sem,
    own_send,
    side_send,
    relay_send,
    fwd_send,
    raw_recv,
    xy_send,
    xy_recv,
    zp_send,
    zp_recv,
    sib_send,
    sib_recv,
    lvl_send,
    lvl_recv,
):
    n_z, n_chip, cap, heads, size = sizes
    half = heads // 2
    length = moe_ref.shape[0]
    width = moe_ref.shape[1]
    c, z = lax.axis_index("ctx"), lax.axis_index("exp")
    core = c % 2
    chip = c // 2
    xbit, ybit = chip % 2, chip // 2
    sib = c + 1 - 2 * core
    xpart = c + 2 - 4 * xbit
    ypart = c + 4 - 8 * ybit
    upper_half, odd = z // 2, z % 2
    partner = z + 1 - 2 * odd
    across = n_z - 1 - z
    inner = odd + upper_half - 2 * odd * upper_half
    toward = z + 1 - 2 * upper_half

    def chip_at(d):
        return (chip + d) % n_chip

    moe_copy = pltpu.make_async_copy(moe_ref, raw.at[z], moe_sem)
    moe_copy.start()
    in_copies = [
        pltpu.make_async_copy(src, dst, in_sem.at[i])
        for i, (src, dst) in enumerate(
            ((k_hbm, k_ref), (v_hbm, v_ref), (q_hbm, q_ref), (g_hbm, g_ref))
        )
    ]
    for copy in in_copies:
        copy.start()

    barrier = pltpu.get_barrier_semaphore()
    for d in range(1, n_chip):
        pl.semaphore_signal(
            barrier, inc=1, device_id={"ctx": chip_at(d) * 2 + core}, device_id_type=MESH
        )
    pl.semaphore_signal(barrier, inc=1, device_id={"ctx": sib}, device_id_type=MESH)

    pl.semaphore_signal(barrier, inc=1, device_id={"exp": partner}, device_id_type=MESH)

    @pl.when(inner == 1)
    def _():
        pl.semaphore_signal(barrier, inc=1, device_id={"exp": across}, device_id_type=MESH)

    pl.semaphore_wait(barrier, n_chip + 1 + inner)

    def raw_copy(src, s, send_sem, to):
        return pltpu.make_async_remote_copy(
            src_ref=src,
            dst_ref=raw.at[s],
            send_sem=send_sem,
            recv_sem=raw_recv.at[s],
            device_id={"exp": to},
            device_id_type=MESH,
        )

    own_copy = raw_copy(moe_ref, z, own_send, toward)
    own_copy.start()
    part = width // 2
    low, high = pl.ds(0, part), pl.ds(part, part)

    def side_copy(s):
        return pltpu.make_async_remote_copy(
            src_ref=moe_ref.at[:, low],
            dst_ref=raw.at[s, :, low],
            send_sem=side_send,
            recv_sem=raw_recv.at[s],
            device_id={"exp": partner},
            device_id_type=MESH,
        )

    @pl.when(inner == 1)
    def _():
        side_copy(z).start()

    relay_copy = raw_copy(raw.at[partner], partner, relay_send, across)

    w_copies = [
        pltpu.make_async_copy(w_hbm.at[0, :, pl.ds(i * width, width)], wbuf.at[i], w_sem.at[i])
        for i in range(n_z)
    ]
    for copy in w_copies:
        copy.start()

    def chunk_at(i):
        return 1 + i + upper_half * (1 - 2 * i) if i else z

    def forward_copy(i):
        s = chunk_at(i)
        return raw_copy(raw.at[s], s, fwd_send.at[i], partner)

    ids = ids_ref[...]
    gates = gate_ref[...]
    expert = lax.broadcasted_iota(jnp.int32, (8, length), 0)
    first, second = ids[0:1, :] == expert, ids[1:2, :] == expert
    named_row = (first | second).astype(jnp.float32)
    weight_row = jnp.where(first, gates[0:1, :], 0.0) + jnp.where(second, gates[1:2, :], 0.0)
    t_row = lax.broadcasted_iota(jnp.int32, (length, length), 0)
    t_col = lax.broadcasted_iota(jnp.int32, (length, length), 1)
    earlier = (t_row < t_col).astype(jnp.float32)
    rank_row = mm(named_row, earlier, NN)
    slot = lax.broadcasted_iota(jnp.int32, (cap, length), 0).astype(jnp.float32)
    for e in range(n_chip):
        hit = (rank_row[e : e + 1, :] == slot) & (named_row[e : e + 1, :] > 0.5)
        table[e] = hit.astype(jnp.float32).astype(jnp.bfloat16)
        gate = jnp.sum(jnp.where(hit, weight_row[e : e + 1, :], 0.0), axis=1, keepdims=True)
        slot_gate[e] = jnp.broadcast_to(gate, (cap, 128))
    for d in range(n_chip):
        near_table[pl.ds(d * cap, cap), :] = table[chip_at(d)]

    def block_of(s, b, i):
        return rows.at[s, b, :, low] if i == n_z - 1 else rows.at[s, b]

    def sent(i, d):
        return sendbuf.at[i, d - 1, :, low] if i == n_z - 1 else sendbuf.at[i, d - 1]

    def xy_copy(i, s, d):
        return pltpu.make_async_remote_copy(
            src_ref=sent(i, d),
            dst_ref=block_of(s, c, i),
            send_sem=xy_send.at[i, d],
            recv_sem=xy_recv.at[s, chip],
            device_id={"ctx": chip_at(d) * 2 + core},
            device_id_type=MESH,
        )

    def xy_arrival(i, s, d):
        source = chip_at(d)
        return pltpu.make_async_remote_copy(
            src_ref=sent(i, d),
            dst_ref=block_of(s, source * 2 + core, i),
            send_sem=xy_send.at[i, d],
            recv_sem=xy_recv.at[s, source],
            device_id={"ctx": source * 2 + core},
            device_id_type=MESH,
        )

    def sib_copy(s, d):
        block = rows.at[s, chip_at(d) * 2 + core]
        return pltpu.make_async_remote_copy(
            src_ref=block,
            dst_ref=block,
            send_sem=sib_send.at[s, d],
            recv_sem=sib_recv.at[s, d],
            device_id={"ctx": sib},
            device_id_type=MESH,
        )

    def sib_arrival(s, d):
        block = rows.at[s, chip_at(d) * 2 + 1 - core]
        return pltpu.make_async_remote_copy(
            src_ref=block,
            dst_ref=block,
            send_sem=sib_send.at[s, d],
            recv_sem=sib_recv.at[s, d],
            device_id={"ctx": sib},
            device_id_type=MESH,
        )

    def zp_copy(s, d):
        block = rows.at[s, chip_at(d) * 2 + core, :, high]
        return pltpu.make_async_remote_copy(
            src_ref=block,
            dst_ref=block,
            send_sem=zp_send.at[d],
            recv_sem=zp_recv.at[d],
            device_id={"exp": partner},
            device_id_type=MESH,
        )

    def take(i):
        forward_copy(i).wait_recv()

        @pl.when(inner == 1)
        def _():
            forward_copy(i).start()

    def route_chunk(i):
        half_only = i == n_z - 1
        s = partner if half_only else chunk_at(i)
        step = part // 2 if (part // 2) % 128 == 0 else part
        for at in range(0, part if half_only else width, step):
            cols = pl.ds(at, step)
            picked = mm(near_table[...], raw[s, :, cols], NN)
            for d in range(n_chip):
                gate = slot_gate[chip_at(d)][:, 0:1]
                routed = (picked[d * cap : (d + 1) * cap, :] * gate).astype(jnp.bfloat16)
                if d:
                    sendbuf[i, d - 1, :, cols] = routed
                else:
                    rows[s, c, :, cols] = routed
        for d in range(1, n_chip):
            xy_copy(i, s, d).start()
        if not half_only:
            sib_copy(s, 0).start()

    def pass_on(i):
        s = chunk_at(i)
        for d in range(1, n_chip):
            xy_arrival(i, s, d).wait_recv()
            sib_copy(s, d).start()

    def hid_copy(j):
        return pltpu.make_async_copy(
            hid.at[j],
            hid_hbm.at[0, pl.ds(pl.multiple_of(j * 2 * cap, 2 * cap), 2 * cap), :],
            hid_sem.at[j],
        )

    def multiply(s, first=False, last=False):
        if first:
            for copy in w_copies:
                copy.wait()

        def tile(j):
            left = rows[s, pl.ds(2 * j, 2)].reshape(2 * cap, width)
            total = mm(left, wbuf[s], NT)
            if not first:
                total = total + acc[j]
            if last:
                hid[j] = total.astype(jnp.bfloat16)
                hid_copy(j).start()
            else:
                acc[j] = total

        for d in range(n_chip):
            sib_arrival(s, d).wait_recv()
            tile(chip_at(d))

    moe_copy.wait()
    route_chunk(0)

    log_decay = ld_ref[...]
    highest = lax.Precision.HIGHEST
    lower = (t_row >= t_col).astype(jnp.float32)
    upper = (t_row <= t_col).astype(jnp.float32)
    running = mm(lower, log_decay, NT, highest)
    running_t = mm(log_decay, upper, NN, highest)
    closing = mm(log_decay, jnp.ones((length, size), jnp.float32), NN, highest)
    for h in range(heads):
        run_col[h] = jnp.broadcast_to(running[:, h : h + 1], (length, size))
        run_row[h] = jnp.broadcast_to(running_t[h : h + 1, :], (8, length))
        close_row[h] = jnp.broadcast_to(closing[h : h + 1, :], (8, size))
        own_decay[h] = jnp.broadcast_to(jnp.exp(closing[h : h + 1, :]), (8, size))

    group = 4 if heads % 4 == 0 else 2

    def per_head(body):
        def turn(i, carry):
            for u in range(group):
                h = i * group + u
                body(h, pl.ds(pl.multiple_of(h * size, size), size))
            return carry

        lax.fori_loop(0, heads // group, turn, 0)

    def block_states(h, cols):
        along = run_col[h]
        until = jnp.exp(close_row[h][0:1, :] - along)
        since = jnp.exp(along)
        key_high, key_low = split_bf16(k_ref[:, cols].astype(jnp.float32) * until)
        query_high, query_low = split_bf16(q_ref[:, cols].astype(jnp.float32) * since)
        value, grad = v_ref[:, cols], g_ref[:, cols]
        state[0, h] = mm(key_high, value, TN) + mm(key_low, value, TN)
        state[1, h] = mm(query_high, grad, TN) + mm(query_low, grad, TN)

    for copy in in_copies:
        copy.wait()
    per_head(block_states)

    def level(index, src, dst, peer):
        return pltpu.make_async_remote_copy(
            src_ref=src,
            dst_ref=dst,
            send_sem=lvl_send.at[index],
            recv_sem=lvl_recv.at[index],
            device_id={"ctx": peer},
            device_id_type=MESH,
        )

    core_state = level(0, state, sib_state, sib)
    core_decay = level(1, own_decay, sib_decay, sib)
    x_state = level(2, chip_state, far_state, xpart)
    x_decay = level(3, chip_decay, far_decay, xpart)
    y_copy = level(4, pair_state.at[ybit], y_state, ypart)
    outer_copy = level(5, outer.at[core], outer.at[core], sib)
    outer_arrival = level(5, outer.at[1 - core], outer.at[1 - core], sib)
    core_state.start()
    core_decay.start()

    def local_parts(h, cols):
        mask = causal_mask(length)
        spread = run_col[h] - run_row[h][0:1, :]
        weights = jnp.where(mask, jnp.exp(jnp.where(mask, spread, 0.0)), 0.0)
        query, key, value, grad = q_ref[:, cols], k_ref[:, cols], v_ref[:, cols], g_ref[:, cols]
        grad_scores = (mm(grad, value, NT) * weights).astype(jnp.bfloat16)
        scores = (mm(query, key, NT) * weights).astype(jnp.bfloat16)
        local[0, :, cols] = mm(grad_scores, key, NN)
        local[1, :, cols] = mm(grad_scores, query, TN)
        local[2, :, cols] = mm(scores, grad, TN)

    @pl.when(inner == 1)
    def _():
        relay_copy.wait_recv()
        relay_copy.start()

    @pl.when(inner == 0)
    def _():
        side_copy(partner).wait_recv()

    route_chunk(n_z - 1)

    core_state.wait_recv()
    core_decay.wait_recv()
    chip_decay[...] = own_decay[...] * sib_decay[...]

    def chip_totals(j, carry):
        h = core * half + j
        mine, theirs = own_decay[h][0:1, :], sib_decay[h][0:1, :]
        s_mine, s_sib = state[0, h], sib_state[0, h]
        g_mine, g_sib = state[1, h], sib_state[1, h]
        first_core = core == 0
        chip_state[0, j] = jnp.where(
            first_core, s_sib + theirs * s_mine, s_mine + mine * s_sib
        ).astype(jnp.bfloat16)
        chip_state[1, j] = jnp.where(
            first_core, g_mine + mine * g_sib, g_sib + theirs * g_mine
        ).astype(jnp.bfloat16)
        return carry

    lax.fori_loop(0, half, chip_totals, 0)
    x_state.start()
    x_decay.start()

    take(1)
    route_chunk(1)
    pass_on(0)

    def send_high():
        for d in range(n_chip):
            zp_copy(z, d).start()

    pl.when(inner == 0)(send_high)
    per_head(local_parts)
    take(2)
    pl.when(inner == 1)(send_high)
    route_chunk(2)
    multiply(z, first=True)

    x_state.wait_recv()
    x_decay.wait_recv()

    def pair_totals(j, carry):
        h = core * half + j
        mine, theirs = chip_decay[h][0:1, :], far_decay[h][0:1, :]
        s_mine, s_far = chip_state[0, j].astype(jnp.float32), far_state[0, j].astype(jnp.float32)
        g_mine, g_far = chip_state[1, j].astype(jnp.float32), far_state[1, j].astype(jnp.float32)
        first_x = xbit == 0
        pair_state[0, j] = jnp.where(
            first_x, s_far + theirs * s_mine, s_mine + mine * s_far
        ).astype(jnp.bfloat16)
        pair_state[1, j] = jnp.where(
            first_x, g_mine + mine * g_far, g_far + theirs * g_mine
        ).astype(jnp.bfloat16)
        return carry

    lax.fori_loop(0, half, pair_totals, 0)
    y_copy.start()

    pass_on(1)
    multiply(chunk_at(1))

    y_copy.wait_recv()

    def outer_states(j, carry):
        h = core * half + j
        theirs = far_decay[h][0:1, :]
        from_y = y_state[j].astype(jnp.float32)
        zero = jnp.zeros_like(from_y)
        y_prefix = jnp.where(ybit == 1, from_y, zero)
        y_suffix = jnp.where(ybit == 0, from_y, zero)
        s_far, g_far = far_state[0, j].astype(jnp.float32), far_state[1, j].astype(jnp.float32)
        outer[core, 0, j] = jnp.where(xbit == 1, s_far + theirs * y_prefix, y_prefix)
        outer[core, 1, j] = jnp.where(xbit == 0, g_far + theirs * y_suffix, y_suffix)
        return carry

    lax.fori_loop(0, half, outer_states, 0)
    outer_copy.start()

    outer_arrival.wait_recv()

    def finish(h, cols):
        along = run_col[h]
        until = jnp.exp(close_row[h][0:1, :] - along)
        since = jnp.exp(along)
        theirs = sib_decay[h][0:1, :]
        side, j = h // half, h % half
        before, after = outer[side, 0, j], outer[side, 1, j]
        prefix = jnp.where(core == 1, sib_state[0, h] + theirs * before, before)
        suffix = jnp.where(core == 0, sib_state[1, h] + theirs * after, after)
        prefix_high, prefix_low = split_bf16(prefix)
        suffix_high, suffix_low = split_bf16(suffix)
        key, value, grad = k_ref[:, cols], v_ref[:, cols], g_ref[:, cols]
        query_part = mm(grad, prefix_high, NT) + mm(grad, prefix_low, NT)
        key_part = mm(value, suffix_high, NT) + mm(value, suffix_low, NT)
        value_part = mm(key, suffix_high, NN) + mm(key, suffix_low, NN)
        grads[0, :, cols] = (local[0, :, cols] + since * query_part).astype(jnp.bfloat16)
        grads[1, :, cols] = (local[1, :, cols] + until * key_part).astype(jnp.bfloat16)
        grads[2, :, cols] = (local[2, :, cols] + until * value_part).astype(jnp.bfloat16)

    per_head(finish)
    out_copies = [
        pltpu.make_async_copy(grads.at[i], dst, out_sem.at[i])
        for i, dst in enumerate((qg_hbm, kg_hbm, vg_hbm))
    ]
    for copy in out_copies:
        copy.start()
    pass_on(2)
    multiply(chunk_at(2))
    for d in range(n_chip):
        if d:
            xy_arrival(n_z - 1, partner, d).wait_recv()
        zp_copy(partner, d).wait_recv()
        sib_copy(partner, d).start()
    multiply(partner, last=True)
    for copy in out_copies:
        copy.wait()
    for j in range(n_chip):
        hid_copy(j).wait()

    own_copy.wait_send()

    @pl.when(inner == 1)
    def _():
        relay_copy.wait_send()
        side_copy(z).wait_send()
        for i in range(1, n_z - 1):
            forward_copy(i).wait_send()

    for i in range(n_z - 1):
        s = chunk_at(i)
        for d in range(1, n_chip):
            xy_copy(i, s, d).wait_send()
        for d in range(n_chip):
            sib_copy(s, d).wait_send()
    for d in range(1, n_chip):
        xy_copy(n_z - 1, partner, d).wait_send()
    for d in range(n_chip):
        zp_copy(z, d).wait_send()
        sib_copy(partner, d).wait_send()
    for copy in (core_state, core_decay, x_state, x_decay, y_copy, outer_copy):
        copy.wait_send()


def hand_over(*refs):
    sems = refs[-1]
    copies = [pltpu.make_async_copy(refs[i], refs[4 + i], sems.at[i]) for i in range(4)]
    for copy in copies:
        copy.start()
    for copy in copies:
        copy.wait()


def fused(
    queries, keys, values, out_grad, log_decay, moe_grad, expert_ids, gate_weights, down_weight
):
    n_ctx, n_z = lax.axis_size("ctx"), lax.axis_size("exp")
    n_chip = n_ctx // 2
    length, heads = log_decay.shape
    width = moe_grad.shape[1]
    size = queries.shape[1] // heads
    cap = 5 * length // (2 * n_chip)
    half = heads // 2
    hidden = down_weight.shape[1]
    bf16, f32 = jnp.bfloat16, jnp.float32
    dma = pltpu.SemaphoreType.DMA
    vmem = pl.BlockSpec(memory_space=pltpu.VMEM)
    hbm = pl.BlockSpec(memory_space=pl.ANY)
    decay = pltpu.VMEM((heads, 8, size), f32)
    scratch = [
        *[pltpu.VMEM((length, heads * size), bf16)] * 4,
        pltpu.VMEM((3, length, heads * size), bf16),
        pltpu.VMEM((n_chip, 2 * cap, hidden), bf16),
        pltpu.VMEM((n_z, hidden, width), bf16),
        pltpu.VMEM((n_z, length, width), bf16),
        pltpu.VMEM((n_z, n_chip - 1, cap, width), bf16),
        pltpu.VMEM((n_z, n_ctx, cap, width), bf16),
        pltpu.VMEM((n_chip, 2 * cap, hidden), f32),
        pltpu.VMEM((n_chip, cap, length), bf16),
        pltpu.VMEM((n_chip * cap, length), bf16),
        pltpu.VMEM((n_chip, cap, 128), f32),
        pltpu.VMEM((heads, length, size), f32),
        pltpu.VMEM((heads, 8, length), f32),
        decay,
        decay,
        decay,
        decay,
        decay,
        pltpu.VMEM((2, heads, size, size), f32),
        pltpu.VMEM((2, heads, size, size), f32),
        pltpu.VMEM((2, half, size, size), bf16),
        pltpu.VMEM((2, half, size, size), bf16),
        pltpu.VMEM((2, half, size, size), bf16),
        pltpu.VMEM((half, size, size), bf16),
        pltpu.VMEM((2, 2, half, size, size), f32),
        pltpu.VMEM((3, length, width), f32),
        dma((4,)),
        dma((3,)),
        dma((n_chip,)),
        dma,
        dma((n_z,)),
        dma,
        dma,
        dma,
        dma((n_z - 1,)),
        dma((n_z,)),
        dma((n_z, n_chip)),
        dma((n_z, n_chip)),
        dma((n_chip,)),
        dma((n_chip,)),
        dma((n_z, n_chip)),
        dma((n_z, n_chip)),
        dma((6,)),
        dma((6,)),
    ]
    flat = jax.ShapeDtypeStruct((length, heads * size), bf16)
    results = pl.pallas_call(
        functools.partial(fused_kernel, (n_z, n_chip, cap, heads, size)),
        out_shape=(
            flat,
            flat,
            flat,
            jax.ShapeDtypeStruct((1, n_ctx * cap, hidden), bf16),
        ),
        in_specs=[hbm] * 4 + [vmem, hbm, vmem, vmem, hbm],
        out_specs=(hbm,) * 4,
        scratch_shapes=scratch,
        compiler_params=pltpu.CompilerParams(
            collective_id=0, has_side_effects=True, vmem_limit_bytes=60 * 2**20
        ),
    )(
        queries,
        keys,
        values,
        out_grad,
        log_decay.T,
        moe_grad,
        expert_ids.T,
        gate_weights.T,
        down_weight,
    )
    return pl.pallas_call(
        hand_over,
        out_shape=tuple(jax.ShapeDtypeStruct(x.shape, x.dtype) for x in results),
        in_specs=[hbm] * 4,
        out_specs=(hbm,) * 4,
        scratch_shapes=[dma((4,))],
        compiler_params=pltpu.CompilerParams(vmem_limit_bytes=60 * 2**20),
    )(*results)


def body(
    queries, keys, values, out_grad, log_decay, moe_grad, expert_ids, gate_weights, down_weight
):
    n_ctx, n_z = lax.axis_size("ctx"), lax.axis_size("exp")
    length, heads = log_decay.shape
    cap = 5 * length // n_ctx
    args = (
        queries, keys, values, out_grad, log_decay, moe_grad, expert_ids, gate_weights, down_weight
    )
    size = queries.shape[1] // heads
    fits = (
        n_ctx == 8
        and n_z == 4
        and cap % 16 == 0
        and size == 128
        and length == 128
        and heads % 2 == 0
        and moe_grad.shape[1] % 256 == 0
        and queries.shape[1] == moe_grad.shape[1]
    )
    return fused(*args) if fits else per_device(*args)


def solution(mesh):
    in_specs = (
        P("ctx", "exp"),
        P("ctx", "exp"),
        P("ctx", "exp"),
        P("ctx", "exp"),
        P("ctx", "exp"),
        P("ctx", "exp"),
        P("ctx", None),
        P("ctx", None),
        P("ctx", "exp", None),
    )
    out_specs = (P("ctx", "exp"), P("ctx", "exp"), P("ctx", "exp"), P("ctx", None, "exp"))
    return jax.shard_map(
        body, mesh=mesh, in_specs=in_specs, out_specs=out_specs, check_vma=False
    )
```

```python
import functools

import jax
import jax.numpy as jnp
from jax import lax
from jax.experimental import pallas as pl
from jax.experimental.pallas import tpu as pltpu
from jax.sharding import PartitionSpec as P


def carried_in(x, axis, combine, identity, reverse):
    devices, place = (lax.axis_size(axis), lax.axis_index(axis))
    everything = jax.tree.map(lambda part: lax.all_gather(part, axis), x)
    start = jax.tree.map(
        lambda part, zero: jnp.broadcast_to(jnp.asarray(zero, part.dtype), part.shape), x, identity
    )

    def turn(k, before):
        at = devices - 1 - k if reverse else k
        reached = at > place if reverse else at < place
        new = combine(before, jax.tree.map(lambda part: part[at], everything))
        return jax.tree.map(lambda a, b: jnp.where(reached, a, b), new, before)

    return lax.fori_loop(0, devices, turn, start)


def partner_2(value, axis, apart):
    mask = 2**apart
    pairs = [(source, source ^ mask) for source in range(lax.axis_size(axis))]
    return lax.ppermute(value, axis, pairs)


def combine_states(earlier, later):
    return (later[1][:, None, None] * earlier[0] + later[0], earlier[1] * later[1])


def attention_grads(queries, keys, values, out_grad, log_decay):
    length, head_count = log_decay.shape
    head_size = queries.shape[1] // head_count
    query_h = queries.reshape(length, head_count, head_size)
    key_h = keys.reshape(length, head_count, head_size)
    value_h = values.reshape(length, head_count, head_size)
    grad_h = out_grad.reshape(length, head_count, head_size)
    running = jnp.cumsum(log_decay, axis=0)
    closing = running[-1]
    causal = jnp.arange(length)[:, None] >= jnp.arange(length)[None, :]
    spread = running.T[:, :, None] - running.T[:, None, :]
    weights = jnp.where(causal[None], jnp.exp(jnp.where(causal[None], spread, 0.0)), 0.0)
    until_finish = jnp.exp(closing[None, :] - running)
    since_beginning = jnp.exp(running)
    query_full = query_h.astype(jnp.float32)
    key_full = key_h.astype(jnp.float32)
    value_full = value_h.astype(jnp.float32)
    gradient_full = grad_h.astype(jnp.float32)
    block_state = jnp.einsum(
        "jqz,jqb->qzb",
        key_full * until_finish[:, :, None],
        value_full,
        precision=lax.Precision.HIGHEST,
    )
    block_grad = jnp.einsum(
        "soj,sop->ojp",
        query_full * since_beginning[:, :, None],
        gradient_full,
        precision=lax.Precision.HIGHEST,
    )
    block_decay = jnp.exp(closing)
    identity_pair = (jnp.zeros_like(block_state), jnp.ones_like(block_decay))
    leading_part, _ = carried_in(
        (block_state, block_decay), "ctx", combine_states, identity_pair, False
    )
    trailing_part, _ = carried_in(
        (block_grad, block_decay), "ctx", combine_states, identity_pair, True
    )
    grad_scores = (
        jnp.einsum("thv,shv->hts", grad_h, value_h, preferred_element_type=jnp.float32) * weights
    ).astype(jnp.bfloat16)
    scores = (
        jnp.einsum("thk,shk->hts", query_h, key_h, preferred_element_type=jnp.float32) * weights
    ).astype(jnp.bfloat16)
    query_grad = jnp.einsum(
        "hts,shk->thk", grad_scores, key_h, preferred_element_type=jnp.float32
    ) + since_beginning[:, :, None] * jnp.einsum(
        "xrq,rgq->xrg", gradient_full, leading_part, precision=lax.Precision.HIGHEST
    )
    key_grad = jnp.einsum(
        "hts,thk->shk", grad_scores, query_h, preferred_element_type=jnp.float32
    ) + until_finish[:, :, None] * jnp.einsum(
        "pox,ofx->pof", value_full, trailing_part, precision=lax.Precision.HIGHEST
    )
    value_grad = jnp.einsum(
        "hts,thv->shv", scores, grad_h, preferred_element_type=jnp.float32
    ) + until_finish[:, :, None] * jnp.einsum(
        "raj,ajb->rab", key_full, trailing_part, precision=lax.Precision.HIGHEST
    )
    flat_width = head_count * head_size
    return (
        query_grad.reshape(length, flat_width).astype(jnp.bfloat16),
        key_grad.reshape(length, flat_width).astype(jnp.bfloat16),
        value_grad.reshape(length, flat_width).astype(jnp.bfloat16),
    )


def route_rows(moe_grad, expert_ids, gate_weights, experts, capacity):
    pair_ids = expert_ids.reshape(-1)
    onehot = (pair_ids[:, None] == jnp.arange(experts)[None, :]).astype(jnp.int32)
    earlier = jnp.cumsum(onehot, axis=0) - onehot
    pair_slots = (pair_ids * capacity + jnp.sum(earlier * onehot, axis=1)).reshape(-1, 2)
    slot_iota = jnp.arange(experts * capacity)[:, None]
    first_table = jnp.where(
        slot_iota == pair_slots[:, 0][None, :], gate_weights[:, 0][None, :], 0.0
    )
    second_table = jnp.where(
        slot_iota == pair_slots[:, 1][None, :], gate_weights[:, 1][None, :], 0.0
    )
    dispatch_table = first_table + second_table
    return jnp.dot(
        dispatch_table, moe_grad.astype(jnp.float32), precision=lax.Precision.HIGHEST
    ).astype(jnp.bfloat16)


def per_device(
    queries, keys, values, out_grad, log_decay, moe_grad, expert_ids, gate_weights, down_weight
):
    query_grad, key_grad, value_grad = attention_grads(queries, keys, values, out_grad, log_decay)
    devices_ctx = lax.axis_size("ctx")
    experts = devices_ctx // 2
    length = moe_grad.shape[0]
    capacity = 5 * length // (2 * experts)
    routed = route_rows(moe_grad, expert_ids, gate_weights, experts, capacity)
    weight_slab = down_weight[0]
    half_count = capacity // 2
    own_rows = lax.all_to_all(routed, "ctx", split_axis=0, concat_axis=0, tiled=True)
    own_full = lax.all_gather(own_rows, "exp", axis=1, tiled=True)
    partner = partner_2(own_full, "ctx", 0)
    parity = lax.axis_index("ctx") % 2
    own_view = own_full.reshape(devices_ctx, half_count, -1)
    partner_view = partner.reshape(devices_ctx, half_count, -1)
    lower_half = jnp.where(parity == 0, own_view, partner_view)
    upper_half = jnp.where(parity == 0, partner_view, own_view)
    all_rows = jnp.concatenate([lower_half, upper_half], axis=1).reshape(devices_ctx * capacity, -1)
    hidden = jnp.einsum("sd,fd->sf", all_rows, weight_slab, preferred_element_type=jnp.float32)
    hidden_grad = hidden.astype(jnp.bfloat16)[None]
    return (query_grad, key_grad, value_grad, hidden_grad)


MESH = pl.DeviceIdType.MESH
NT = (((1,), (1,)), ((), ()))
NN = (((1,), (0,)), ((), ()))
TN = (((0,), (0,)), ((), ()))


def mm(a, b, dims, precision=None):
    return lax.dot_general(a, b, dims, precision=precision, preferred_element_type=jnp.float32)


def split_bf16(x):
    high = x.astype(jnp.bfloat16)
    return high, (x - high.astype(jnp.float32)).astype(jnp.bfloat16)


def causal_mask(size):
    return lax.broadcasted_iota(jnp.int32, (size, size), 0) >= lax.broadcasted_iota(
        jnp.int32, (size, size), 1
    )


def fused_kernel(
    sizes,
    q_hbm,
    k_hbm,
    v_hbm,
    g_hbm,
    ld_ref,
    moe_ref,
    ids_ref,
    gate_ref,
    w_hbm,
    qg_hbm,
    kg_hbm,
    vg_hbm,
    hid_hbm,
    q_ref,
    k_ref,
    v_ref,
    g_ref,
    grads,
    hid,
    wbuf,
    raw,
    sendbuf,
    rows,
    acc,
    table,
    near_table,
    slot_gate,
    run_col,
    run_row,
    close_row,
    own_decay,
    sib_decay,
    chip_decay,
    far_decay,
    state,
    sib_state,
    chip_state,
    far_state,
    pair_state,
    y_state,
    outer,
    local,
    in_sem,
    out_sem,
    hid_sem,
    moe_sem,
    w_sem,
    own_send,
    side_send,
    relay_send,
    fwd_send,
    raw_recv,
    xy_send,
    xy_recv,
    zp_send,
    zp_recv,
    sib_send,
    sib_recv,
    lvl_send,
    lvl_recv,
):
    n_z, n_chip, cap, heads, size = sizes
    half = heads // 2
    length = moe_ref.shape[0]
    width = moe_ref.shape[1]
    c, z = lax.axis_index("ctx"), lax.axis_index("exp")
    core = c % 2
    chip = c // 2
    xbit, ybit = chip % 2, chip // 2
    sib = c + 1 - 2 * core
    xpart = c + 2 - 4 * xbit
    ypart = c + 4 - 8 * ybit
    upper_half, odd = z // 2, z % 2
    partner = z + 1 - 2 * odd
    across = n_z - 1 - z
    inner = odd + upper_half - 2 * odd * upper_half
    toward = z + 1 - 2 * upper_half

    def chip_at(d):
        return (chip + d) % n_chip

    moe_copy = pltpu.make_async_copy(moe_ref, raw.at[z], moe_sem)
    moe_copy.start()
    in_copies = [
        pltpu.make_async_copy(src, dst, in_sem.at[i])
        for i, (src, dst) in enumerate(
            ((k_hbm, k_ref), (v_hbm, v_ref), (q_hbm, q_ref), (g_hbm, g_ref))
        )
    ]
    for copy in in_copies:
        copy.start()

    barrier = pltpu.get_barrier_semaphore()
    for d in range(1, n_chip):
        pl.semaphore_signal(
            barrier, inc=1, device_id={"ctx": chip_at(d) * 2 + core}, device_id_type=MESH
        )
    pl.semaphore_signal(barrier, inc=1, device_id={"ctx": sib}, device_id_type=MESH)

    pl.semaphore_signal(barrier, inc=1, device_id={"exp": partner}, device_id_type=MESH)

    @pl.when(inner == 1)
    def _():
        pl.semaphore_signal(barrier, inc=1, device_id={"exp": across}, device_id_type=MESH)

    pl.semaphore_wait(barrier, n_chip + 1 + inner)

    def raw_copy(src, s, send_sem, to):
        return pltpu.make_async_remote_copy(
            src_ref=src,
            dst_ref=raw.at[s],
            send_sem=send_sem,
            recv_sem=raw_recv.at[s],
            device_id={"exp": to},
            device_id_type=MESH,
        )

    own_copy = raw_copy(moe_ref, z, own_send, toward)
    own_copy.start()
    part = width // 2
    low, high = pl.ds(0, part), pl.ds(part, part)

    def side_copy(s):
        return pltpu.make_async_remote_copy(
            src_ref=moe_ref.at[:, low],
            dst_ref=raw.at[s, :, low],
            send_sem=side_send,
            recv_sem=raw_recv.at[s],
            device_id={"exp": partner},
            device_id_type=MESH,
        )

    @pl.when(inner == 1)
    def _():
        side_copy(z).start()

    relay_copy = raw_copy(raw.at[partner], partner, relay_send, across)

    w_copies = [
        pltpu.make_async_copy(w_hbm.at[0, :, pl.ds(i * width, width)], wbuf.at[i], w_sem.at[i])
        for i in range(n_z)
    ]
    for copy in w_copies:
        copy.start()

    def chunk_at(i):
        return 1 + i + upper_half * (1 - 2 * i) if i else z

    def forward_copy(i):
        s = chunk_at(i)
        return raw_copy(raw.at[s], s, fwd_send.at[i], partner)

    ids = ids_ref[...]
    gates = gate_ref[...]
    expert = lax.broadcasted_iota(jnp.int32, (8, length), 0)
    first, second = ids[0:1, :] == expert, ids[1:2, :] == expert
    named_row = (first | second).astype(jnp.float32)
    weight_row = jnp.where(first, gates[0:1, :], 0.0) + jnp.where(second, gates[1:2, :], 0.0)
    t_row = lax.broadcasted_iota(jnp.int32, (length, length), 0)
    t_col = lax.broadcasted_iota(jnp.int32, (length, length), 1)
    earlier = (t_row < t_col).astype(jnp.float32)
    rank_row = mm(named_row, earlier, NN)
    slot = lax.broadcasted_iota(jnp.int32, (cap, length), 0).astype(jnp.float32)
    for e in range(n_chip):
        hit = (rank_row[e : e + 1, :] == slot) & (named_row[e : e + 1, :] > 0.5)
        table[e] = hit.astype(jnp.float32).astype(jnp.bfloat16)
        gate = jnp.sum(jnp.where(hit, weight_row[e : e + 1, :], 0.0), axis=1, keepdims=True)
        slot_gate[e] = jnp.broadcast_to(gate, (cap, 128))
    for d in range(n_chip):
        near_table[pl.ds(d * cap, cap), :] = table[chip_at(d)]

    def block_of(s, b, i):
        return rows.at[s, b, :, low] if i == n_z - 1 else rows.at[s, b]

    def sent(i, d):
        return sendbuf.at[i, d - 1, :, low] if i == n_z - 1 else sendbuf.at[i, d - 1]

    def xy_copy(i, s, d):
        return pltpu.make_async_remote_copy(
            src_ref=sent(i, d),
            dst_ref=block_of(s, c, i),
            send_sem=xy_send.at[i, d],
            recv_sem=xy_recv.at[s, chip],
            device_id={"ctx": chip_at(d) * 2 + core},
            device_id_type=MESH,
        )

    def xy_arrival(i, s, d):
        source = chip_at(d)
        return pltpu.make_async_remote_copy(
            src_ref=sent(i, d),
            dst_ref=block_of(s, source * 2 + core, i),
            send_sem=xy_send.at[i, d],
            recv_sem=xy_recv.at[s, source],
            device_id={"ctx": source * 2 + core},
            device_id_type=MESH,
        )

    def sib_copy(s, d):
        block = rows.at[s, chip_at(d) * 2 + core]
        return pltpu.make_async_remote_copy(
            src_ref=block,
            dst_ref=block,
            send_sem=sib_send.at[s, d],
            recv_sem=sib_recv.at[s, d],
            device_id={"ctx": sib},
            device_id_type=MESH,
        )

    def sib_arrival(s, d):
        block = rows.at[s, chip_at(d) * 2 + 1 - core]
        return pltpu.make_async_remote_copy(
            src_ref=block,
            dst_ref=block,
            send_sem=sib_send.at[s, d],
            recv_sem=sib_recv.at[s, d],
            device_id={"ctx": sib},
            device_id_type=MESH,
        )

    def zp_copy(s, d):
        block = rows.at[s, chip_at(d) * 2 + core, :, high]
        return pltpu.make_async_remote_copy(
            src_ref=block,
            dst_ref=block,
            send_sem=zp_send.at[d],
            recv_sem=zp_recv.at[d],
            device_id={"exp": partner},
            device_id_type=MESH,
        )

    def take(i):
        forward_copy(i).wait_recv()

        @pl.when(inner == 1)
        def _():
            forward_copy(i).start()

    def route_chunk(i):
        half_only = i == n_z - 1
        s = partner if half_only else chunk_at(i)
        step = part // 2 if (part // 2) % 128 == 0 else part
        for at in range(0, part if half_only else width, step):
            cols = pl.ds(at, step)
            picked = mm(near_table[...], raw[s, :, cols], NN)
            for d in range(n_chip):
                gate = slot_gate[chip_at(d)][:, 0:1]
                routed = (picked[d * cap : (d + 1) * cap, :] * gate).astype(jnp.bfloat16)
                if d:
                    sendbuf[i, d - 1, :, cols] = routed
                else:
                    rows[s, c, :, cols] = routed
        for d in range(1, n_chip):
            xy_copy(i, s, d).start()
        if not half_only:
            sib_copy(s, 0).start()

    def pass_on(i):
        s = chunk_at(i)
        for d in range(1, n_chip):
            xy_arrival(i, s, d).wait_recv()
            sib_copy(s, d).start()

    def hid_copy(j):
        return pltpu.make_async_copy(
            hid.at[j],
            hid_hbm.at[0, pl.ds(pl.multiple_of(j * 2 * cap, 2 * cap), 2 * cap), :],
            hid_sem.at[j],
        )

    def multiply(s, first=False, last=False):
        if first:
            for copy in w_copies:
                copy.wait()

        def tile(j):
            left = rows[s, pl.ds(2 * j, 2)].reshape(2 * cap, width)
            total = mm(left, wbuf[s], NT)
            if not first:
                total = total + acc[j]
            if last:
                hid[j] = total.astype(jnp.bfloat16)
                hid_copy(j).start()
            else:
                acc[j] = total

        for d in range(n_chip):
            sib_arrival(s, d).wait_recv()
            tile(chip_at(d))

    moe_copy.wait()
    route_chunk(0)

    log_decay = ld_ref[...]
    highest = lax.Precision.HIGHEST
    lower = (t_row >= t_col).astype(jnp.float32)
    upper = (t_row <= t_col).astype(jnp.float32)
    running = mm(lower, log_decay, NT, highest)
    running_t = mm(log_decay, upper, NN, highest)
    closing = mm(log_decay, jnp.ones((length, size), jnp.float32), NN, highest)
    for h in range(heads):
        run_col[h] = jnp.broadcast_to(running[:, h : h + 1], (length, size))
        run_row[h] = jnp.broadcast_to(running_t[h : h + 1, :], (8, length))
        close_row[h] = jnp.broadcast_to(closing[h : h + 1, :], (8, size))
        own_decay[h] = jnp.broadcast_to(jnp.exp(closing[h : h + 1, :]), (8, size))

    group = 4 if heads % 4 == 0 else 2

    def per_head(body):
        def turn(i, carry):
            for u in range(group):
                h = i * group + u
                body(h, pl.ds(pl.multiple_of(h * size, size), size))
            return carry

        lax.fori_loop(0, heads // group, turn, 0)

    def block_states(h, cols):
        along = run_col[h]
        until = jnp.exp(close_row[h][0:1, :] - along)
        since = jnp.exp(along)
        key_high, key_low = split_bf16(k_ref[:, cols].astype(jnp.float32) * until)
        query_high, query_low = split_bf16(q_ref[:, cols].astype(jnp.float32) * since)
        value, grad = v_ref[:, cols], g_ref[:, cols]
        state[0, h] = mm(key_high, value, TN) + mm(key_low, value, TN)
        state[1, h] = mm(query_high, grad, TN) + mm(query_low, grad, TN)

    for copy in in_copies:
        copy.wait()
    per_head(block_states)

    def level(index, src, dst, peer):
        return pltpu.make_async_remote_copy(
            src_ref=src,
            dst_ref=dst,
            send_sem=lvl_send.at[index],
            recv_sem=lvl_recv.at[index],
            device_id={"ctx": peer},
            device_id_type=MESH,
        )

    core_state = level(0, state, sib_state, sib)
    core_decay = level(1, own_decay, sib_decay, sib)
    x_state = level(2, chip_state, far_state, xpart)
    x_decay = level(3, chip_decay, far_decay, xpart)
    y_copy = level(4, pair_state.at[ybit], y_state, ypart)
    outer_copy = level(5, outer.at[core], outer.at[core], sib)
    outer_arrival = level(5, outer.at[1 - core], outer.at[1 - core], sib)
    core_state.start()
    core_decay.start()

    def local_parts(h, cols):
        mask = causal_mask(length)
        spread = run_col[h] - run_row[h][0:1, :]
        weights = jnp.where(mask, jnp.exp(jnp.where(mask, spread, 0.0)), 0.0)
        query, key, value, grad = q_ref[:, cols], k_ref[:, cols], v_ref[:, cols], g_ref[:, cols]
        grad_scores = (mm(grad, value, NT) * weights).astype(jnp.bfloat16)
        scores = (mm(query, key, NT) * weights).astype(jnp.bfloat16)
        local[0, :, cols] = mm(grad_scores, key, NN)
        local[1, :, cols] = mm(grad_scores, query, TN)
        local[2, :, cols] = mm(scores, grad, TN)

    @pl.when(inner == 1)
    def _():
        relay_copy.wait_recv()
        relay_copy.start()

    @pl.when(inner == 0)
    def _():
        side_copy(partner).wait_recv()

    route_chunk(n_z - 1)

    core_state.wait_recv()
    core_decay.wait_recv()
    chip_decay[...] = own_decay[...] * sib_decay[...]

    def chip_totals(j, carry):
        h = core * half + j
        mine, theirs = own_decay[h][0:1, :], sib_decay[h][0:1, :]
        s_mine, s_sib = state[0, h], sib_state[0, h]
        g_mine, g_sib = state[1, h], sib_state[1, h]
        first_core = core == 0
        chip_state[0, j] = jnp.where(
            first_core, s_sib + theirs * s_mine, s_mine + mine * s_sib
        ).astype(jnp.bfloat16)
        chip_state[1, j] = jnp.where(
            first_core, g_mine + mine * g_sib, g_sib + theirs * g_mine
        ).astype(jnp.bfloat16)
        return carry

    lax.fori_loop(0, half, chip_totals, 0)
    x_state.start()
    x_decay.start()

    take(1)
    route_chunk(1)
    pass_on(0)

    def send_high():
        for d in range(n_chip):
            zp_copy(z, d).start()

    @pl.when(inner == 1)
    def _():
        forward_copy(2).wait_recv()
        forward_copy(2).start()

    send_high()
    per_head(local_parts)

    @pl.when(inner == 0)
    def _():
        forward_copy(2).wait_recv()

    route_chunk(2)
    multiply(z, first=True)

    x_state.wait_recv()
    x_decay.wait_recv()

    def pair_totals(j, carry):
        h = core * half + j
        mine, theirs = chip_decay[h][0:1, :], far_decay[h][0:1, :]
        s_mine, s_far = chip_state[0, j].astype(jnp.float32), far_state[0, j].astype(jnp.float32)
        g_mine, g_far = chip_state[1, j].astype(jnp.float32), far_state[1, j].astype(jnp.float32)
        first_x = xbit == 0
        pair_state[0, j] = jnp.where(
            first_x, s_far + theirs * s_mine, s_mine + mine * s_far
        ).astype(jnp.bfloat16)
        pair_state[1, j] = jnp.where(
            first_x, g_mine + mine * g_far, g_far + theirs * g_mine
        ).astype(jnp.bfloat16)
        return carry

    lax.fori_loop(0, half, pair_totals, 0)
    y_copy.start()

    pass_on(1)
    multiply(chunk_at(1))

    y_copy.wait_recv()

    def outer_states(j, carry):
        h = core * half + j
        theirs = far_decay[h][0:1, :]
        from_y = y_state[j].astype(jnp.float32)
        zero = jnp.zeros_like(from_y)
        y_prefix = jnp.where(ybit == 1, from_y, zero)
        y_suffix = jnp.where(ybit == 0, from_y, zero)
        s_far, g_far = far_state[0, j].astype(jnp.float32), far_state[1, j].astype(jnp.float32)
        outer[core, 0, j] = jnp.where(xbit == 1, s_far + theirs * y_prefix, y_prefix)
        outer[core, 1, j] = jnp.where(xbit == 0, g_far + theirs * y_suffix, y_suffix)
        return carry

    lax.fori_loop(0, half, outer_states, 0)
    outer_copy.start()

    outer_arrival.wait_recv()

    def finish(h, cols):
        along = run_col[h]
        until = jnp.exp(close_row[h][0:1, :] - along)
        since = jnp.exp(along)
        theirs = sib_decay[h][0:1, :]
        side, j = h // half, h % half
        before, after = outer[side, 0, j], outer[side, 1, j]
        prefix = jnp.where(core == 1, sib_state[0, h] + theirs * before, before)
        suffix = jnp.where(core == 0, sib_state[1, h] + theirs * after, after)
        prefix_high, prefix_low = split_bf16(prefix)
        suffix_high, suffix_low = split_bf16(suffix)
        key, value, grad = k_ref[:, cols], v_ref[:, cols], g_ref[:, cols]
        query_part = mm(grad, prefix_high, NT) + mm(grad, prefix_low, NT)
        key_part = mm(value, suffix_high, NT) + mm(value, suffix_low, NT)
        value_part = mm(key, suffix_high, NN) + mm(key, suffix_low, NN)
        grads[0, :, cols] = (local[0, :, cols] + since * query_part).astype(jnp.bfloat16)
        grads[1, :, cols] = (local[1, :, cols] + until * key_part).astype(jnp.bfloat16)
        grads[2, :, cols] = (local[2, :, cols] + until * value_part).astype(jnp.bfloat16)

    per_head(finish)
    out_copies = [
        pltpu.make_async_copy(grads.at[i], dst, out_sem.at[i])
        for i, dst in enumerate((qg_hbm, kg_hbm, vg_hbm))
    ]
    for copy in out_copies:
        copy.start()
    pass_on(2)
    multiply(chunk_at(2))
    for d in range(n_chip):
        if d:
            xy_arrival(n_z - 1, partner, d).wait_recv()
        zp_copy(partner, d).wait_recv()
        sib_copy(partner, d).start()
    multiply(partner, last=True)
    for copy in out_copies:
        copy.wait()
    for j in range(n_chip):
        hid_copy(j).wait()

    own_copy.wait_send()

    @pl.when(inner == 1)
    def _():
        relay_copy.wait_send()
        side_copy(z).wait_send()
        for i in range(1, n_z - 1):
            forward_copy(i).wait_send()

    for i in range(n_z - 1):
        s = chunk_at(i)
        for d in range(1, n_chip):
            xy_copy(i, s, d).wait_send()
        for d in range(n_chip):
            sib_copy(s, d).wait_send()
    for d in range(1, n_chip):
        xy_copy(n_z - 1, partner, d).wait_send()
    for d in range(n_chip):
        zp_copy(z, d).wait_send()
        sib_copy(partner, d).wait_send()
    for copy in (core_state, core_decay, x_state, x_decay, y_copy, outer_copy):
        copy.wait_send()


def hand_over(*refs):
    sources, results, stages, in_sem, out_sem = refs[:4], refs[4:8], refs[8:12], refs[12], refs[13]
    pulls = [pltpu.make_async_copy(sources[i], stages[i], in_sem.at[i]) for i in range(4)]
    pushes = [pltpu.make_async_copy(stages[i], results[i], out_sem.at[i]) for i in range(4)]
    for pull in pulls:
        pull.start()
    for pull, push in zip(pulls, pushes):
        pull.wait()
        push.start()
    for push in pushes:
        push.wait()


def fused(
    queries, keys, values, out_grad, log_decay, moe_grad, expert_ids, gate_weights, down_weight
):
    n_ctx, n_z = lax.axis_size("ctx"), lax.axis_size("exp")
    n_chip = n_ctx // 2
    length, heads = log_decay.shape
    width = moe_grad.shape[1]
    size = queries.shape[1] // heads
    cap = 5 * length // (2 * n_chip)
    half = heads // 2
    hidden = down_weight.shape[1]
    bf16, f32 = jnp.bfloat16, jnp.float32
    dma = pltpu.SemaphoreType.DMA
    vmem = pl.BlockSpec(memory_space=pltpu.VMEM)
    hbm = pl.BlockSpec(memory_space=pl.ANY)
    decay = pltpu.VMEM((heads, 8, size), f32)
    scratch = [
        *[pltpu.VMEM((length, heads * size), bf16)] * 4,
        pltpu.VMEM((3, length, heads * size), bf16),
        pltpu.VMEM((n_chip, 2 * cap, hidden), bf16),
        pltpu.VMEM((n_z, hidden, width), bf16),
        pltpu.VMEM((n_z, length, width), bf16),
        pltpu.VMEM((n_z, n_chip - 1, cap, width), bf16),
        pltpu.VMEM((n_z, n_ctx, cap, width), bf16),
        pltpu.VMEM((n_chip, 2 * cap, hidden), f32),
        pltpu.VMEM((n_chip, cap, length), bf16),
        pltpu.VMEM((n_chip * cap, length), bf16),
        pltpu.VMEM((n_chip, cap, 128), f32),
        pltpu.VMEM((heads, length, size), f32),
        pltpu.VMEM((heads, 8, length), f32),
        decay,
        decay,
        decay,
        decay,
        decay,
        pltpu.VMEM((2, heads, size, size), f32),
        pltpu.VMEM((2, heads, size, size), f32),
        pltpu.VMEM((2, half, size, size), bf16),
        pltpu.VMEM((2, half, size, size), bf16),
        pltpu.VMEM((2, half, size, size), bf16),
        pltpu.VMEM((half, size, size), bf16),
        pltpu.VMEM((2, 2, half, size, size), f32),
        pltpu.VMEM((3, length, width), f32),
        dma((4,)),
        dma((3,)),
        dma((n_chip,)),
        dma,
        dma((n_z,)),
        dma,
        dma,
        dma,
        dma((n_z - 1,)),
        dma((n_z,)),
        dma((n_z, n_chip)),
        dma((n_z, n_chip)),
        dma((n_chip,)),
        dma((n_chip,)),
        dma((n_z, n_chip)),
        dma((n_z, n_chip)),
        dma((6,)),
        dma((6,)),
    ]
    flat = jax.ShapeDtypeStruct((length, heads * size), bf16)
    results = pl.pallas_call(
        functools.partial(fused_kernel, (n_z, n_chip, cap, heads, size)),
        out_shape=(
            flat,
            flat,
            flat,
            jax.ShapeDtypeStruct((1, n_ctx * cap, hidden), bf16),
        ),
        in_specs=[hbm] * 4 + [vmem, hbm, vmem, vmem, hbm],
        out_specs=(hbm,) * 4,
        scratch_shapes=scratch,
        compiler_params=pltpu.CompilerParams(
            collective_id=0, has_side_effects=True, vmem_limit_bytes=60 * 2**20
        ),
    )(
        queries,
        keys,
        values,
        out_grad,
        log_decay.T,
        moe_grad,
        expert_ids.T,
        gate_weights.T,
        down_weight,
    )
    return pl.pallas_call(
        hand_over,
        out_shape=tuple(jax.ShapeDtypeStruct(x.shape, x.dtype) for x in results),
        in_specs=[hbm] * 4,
        out_specs=(hbm,) * 4,
        scratch_shapes=[*[pltpu.VMEM(x.shape, x.dtype) for x in results], dma((4,)), dma((4,))],
        compiler_params=pltpu.CompilerParams(vmem_limit_bytes=60 * 2**20),
    )(*results)


def body(
    queries, keys, values, out_grad, log_decay, moe_grad, expert_ids, gate_weights, down_weight
):
    n_ctx, n_z = lax.axis_size("ctx"), lax.axis_size("exp")
    length, heads = log_decay.shape
    cap = 5 * length // n_ctx
    args = (
        queries, keys, values, out_grad, log_decay, moe_grad, expert_ids, gate_weights, down_weight
    )
    size = queries.shape[1] // heads
    fits = (
        n_ctx == 8
        and n_z == 4
        and cap % 16 == 0
        and size == 128
        and length == 128
        and heads % 2 == 0
        and moe_grad.shape[1] % 256 == 0
        and queries.shape[1] == moe_grad.shape[1]
    )
    return fused(*args) if fits else per_device(*args)


def solution(mesh):
    in_specs = (
        P("ctx", "exp"),
        P("ctx", "exp"),
        P("ctx", "exp"),
        P("ctx", "exp"),
        P("ctx", "exp"),
        P("ctx", "exp"),
        P("ctx", None),
        P("ctx", None),
        P("ctx", "exp", None),
    )
    out_specs = (P("ctx", "exp"), P("ctx", "exp"), P("ctx", "exp"), P("ctx", None, "exp"))
    return jax.shard_map(
        body, mesh=mesh, in_specs=in_specs, out_specs=out_specs, check_vma=False
    )
```

```python
import functools

import jax
import jax.numpy as jnp
from jax import lax
from jax.experimental import pallas as pl
from jax.experimental.pallas import tpu as pltpu
from jax.sharding import PartitionSpec as P


def carried_in(x, axis, combine, identity, reverse):
    devices, place = (lax.axis_size(axis), lax.axis_index(axis))
    everything = jax.tree.map(lambda part: lax.all_gather(part, axis), x)
    start = jax.tree.map(
        lambda part, zero: jnp.broadcast_to(jnp.asarray(zero, part.dtype), part.shape), x, identity
    )

    def turn(k, before):
        at = devices - 1 - k if reverse else k
        reached = at > place if reverse else at < place
        new = combine(before, jax.tree.map(lambda part: part[at], everything))
        return jax.tree.map(lambda a, b: jnp.where(reached, a, b), new, before)

    return lax.fori_loop(0, devices, turn, start)


def partner_2(value, axis, apart):
    mask = 2**apart
    pairs = [(source, source ^ mask) for source in range(lax.axis_size(axis))]
    return lax.ppermute(value, axis, pairs)


def combine_states(earlier, later):
    return (later[1][:, None, None] * earlier[0] + later[0], earlier[1] * later[1])


def attention_grads(queries, keys, values, out_grad, log_decay):
    length, head_count = log_decay.shape
    head_size = queries.shape[1] // head_count
    query_h = queries.reshape(length, head_count, head_size)
    key_h = keys.reshape(length, head_count, head_size)
    value_h = values.reshape(length, head_count, head_size)
    grad_h = out_grad.reshape(length, head_count, head_size)
    running = jnp.cumsum(log_decay, axis=0)
    closing = running[-1]
    causal = jnp.arange(length)[:, None] >= jnp.arange(length)[None, :]
    spread = running.T[:, :, None] - running.T[:, None, :]
    weights = jnp.where(causal[None], jnp.exp(jnp.where(causal[None], spread, 0.0)), 0.0)
    until_finish = jnp.exp(closing[None, :] - running)
    since_beginning = jnp.exp(running)
    query_full = query_h.astype(jnp.float32)
    key_full = key_h.astype(jnp.float32)
    value_full = value_h.astype(jnp.float32)
    gradient_full = grad_h.astype(jnp.float32)
    block_state = jnp.einsum(
        "jqz,jqb->qzb",
        key_full * until_finish[:, :, None],
        value_full,
        precision=lax.Precision.HIGHEST,
    )
    block_grad = jnp.einsum(
        "soj,sop->ojp",
        query_full * since_beginning[:, :, None],
        gradient_full,
        precision=lax.Precision.HIGHEST,
    )
    block_decay = jnp.exp(closing)
    identity_pair = (jnp.zeros_like(block_state), jnp.ones_like(block_decay))
    leading_part, _ = carried_in(
        (block_state, block_decay), "ctx", combine_states, identity_pair, False
    )
    trailing_part, _ = carried_in(
        (block_grad, block_decay), "ctx", combine_states, identity_pair, True
    )
    grad_scores = (
        jnp.einsum("thv,shv->hts", grad_h, value_h, preferred_element_type=jnp.float32) * weights
    ).astype(jnp.bfloat16)
    scores = (
        jnp.einsum("thk,shk->hts", query_h, key_h, preferred_element_type=jnp.float32) * weights
    ).astype(jnp.bfloat16)
    query_grad = jnp.einsum(
        "hts,shk->thk", grad_scores, key_h, preferred_element_type=jnp.float32
    ) + since_beginning[:, :, None] * jnp.einsum(
        "xrq,rgq->xrg", gradient_full, leading_part, precision=lax.Precision.HIGHEST
    )
    key_grad = jnp.einsum(
        "hts,thk->shk", grad_scores, query_h, preferred_element_type=jnp.float32
    ) + until_finish[:, :, None] * jnp.einsum(
        "pox,ofx->pof", value_full, trailing_part, precision=lax.Precision.HIGHEST
    )
    value_grad = jnp.einsum(
        "hts,thv->shv", scores, grad_h, preferred_element_type=jnp.float32
    ) + until_finish[:, :, None] * jnp.einsum(
        "raj,ajb->rab", key_full, trailing_part, precision=lax.Precision.HIGHEST
    )
    flat_width = head_count * head_size
    return (
        query_grad.reshape(length, flat_width).astype(jnp.bfloat16),
        key_grad.reshape(length, flat_width).astype(jnp.bfloat16),
        value_grad.reshape(length, flat_width).astype(jnp.bfloat16),
    )


def route_rows(moe_grad, expert_ids, gate_weights, experts, capacity):
    pair_ids = expert_ids.reshape(-1)
    onehot = (pair_ids[:, None] == jnp.arange(experts)[None, :]).astype(jnp.int32)
    earlier = jnp.cumsum(onehot, axis=0) - onehot
    pair_slots = (pair_ids * capacity + jnp.sum(earlier * onehot, axis=1)).reshape(-1, 2)
    slot_iota = jnp.arange(experts * capacity)[:, None]
    first_table = jnp.where(
        slot_iota == pair_slots[:, 0][None, :], gate_weights[:, 0][None, :], 0.0
    )
    second_table = jnp.where(
        slot_iota == pair_slots[:, 1][None, :], gate_weights[:, 1][None, :], 0.0
    )
    dispatch_table = first_table + second_table
    return jnp.dot(
        dispatch_table, moe_grad.astype(jnp.float32), precision=lax.Precision.HIGHEST
    ).astype(jnp.bfloat16)


def per_device(
    queries, keys, values, out_grad, log_decay, moe_grad, expert_ids, gate_weights, down_weight
):
    query_grad, key_grad, value_grad = attention_grads(queries, keys, values, out_grad, log_decay)
    devices_ctx = lax.axis_size("ctx")
    experts = devices_ctx // 2
    length = moe_grad.shape[0]
    capacity = 5 * length // (2 * experts)
    routed = route_rows(moe_grad, expert_ids, gate_weights, experts, capacity)
    weight_slab = down_weight[0]
    half_count = capacity // 2
    own_rows = lax.all_to_all(routed, "ctx", split_axis=0, concat_axis=0, tiled=True)
    own_full = lax.all_gather(own_rows, "exp", axis=1, tiled=True)
    partner = partner_2(own_full, "ctx", 0)
    parity = lax.axis_index("ctx") % 2
    own_view = own_full.reshape(devices_ctx, half_count, -1)
    partner_view = partner.reshape(devices_ctx, half_count, -1)
    lower_half = jnp.where(parity == 0, own_view, partner_view)
    upper_half = jnp.where(parity == 0, partner_view, own_view)
    all_rows = jnp.concatenate([lower_half, upper_half], axis=1).reshape(devices_ctx * capacity, -1)
    hidden = jnp.einsum("sd,fd->sf", all_rows, weight_slab, preferred_element_type=jnp.float32)
    hidden_grad = hidden.astype(jnp.bfloat16)[None]
    return (query_grad, key_grad, value_grad, hidden_grad)


MESH = pl.DeviceIdType.MESH
NT = (((1,), (1,)), ((), ()))
NN = (((1,), (0,)), ((), ()))
TN = (((0,), (0,)), ((), ()))


def mm(a, b, dims, precision=None):
    return lax.dot_general(a, b, dims, precision=precision, preferred_element_type=jnp.float32)


def split_bf16(x):
    high = x.astype(jnp.bfloat16)
    return high, (x - high.astype(jnp.float32)).astype(jnp.bfloat16)


def causal_mask(size):
    return lax.broadcasted_iota(jnp.int32, (size, size), 0) >= lax.broadcasted_iota(
        jnp.int32, (size, size), 1
    )


def fused_kernel(
    sizes,
    q_hbm,
    k_hbm,
    v_hbm,
    g_hbm,
    ld_ref,
    moe_ref,
    ids_ref,
    gate_ref,
    w_hbm,
    qg_hbm,
    kg_hbm,
    vg_hbm,
    hid_hbm,
    q_ref,
    k_ref,
    v_ref,
    g_ref,
    grads,
    hid,
    wbuf,
    raw,
    sendbuf,
    rows,
    acc,
    table,
    near_table,
    slot_gate,
    run_col,
    run_row,
    close_row,
    own_decay,
    sib_decay,
    chip_decay,
    far_decay,
    state,
    sib_state,
    chip_state,
    far_state,
    pair_state,
    y_state,
    outer,
    local,
    in_sem,
    out_sem,
    hid_sem,
    moe_sem,
    w_sem,
    own_send,
    side_send,
    relay_send,
    fwd_send,
    raw_recv,
    xy_send,
    xy_recv,
    zp_send,
    zp_recv,
    sib_send,
    sib_recv,
    lvl_send,
    lvl_recv,
):
    n_z, n_chip, cap, heads, size = sizes
    half = heads // 2
    length = moe_ref.shape[0]
    width = moe_ref.shape[1]
    c, z = lax.axis_index("ctx"), lax.axis_index("exp")
    core = c % 2
    chip = c // 2
    xbit, ybit = chip % 2, chip // 2
    sib = c + 1 - 2 * core
    xpart = c + 2 - 4 * xbit
    ypart = c + 4 - 8 * ybit
    upper_half, odd = z // 2, z % 2
    partner = z + 1 - 2 * odd
    across = n_z - 1 - z
    inner = odd + upper_half - 2 * odd * upper_half
    toward = z + 1 - 2 * upper_half

    def chip_at(d):
        return (chip + d) % n_chip

    moe_copy = pltpu.make_async_copy(moe_ref, raw.at[z], moe_sem)
    moe_copy.start()
    in_copies = [
        pltpu.make_async_copy(src, dst, in_sem.at[i])
        for i, (src, dst) in enumerate(
            ((k_hbm, k_ref), (v_hbm, v_ref), (q_hbm, q_ref), (g_hbm, g_ref))
        )
    ]
    for copy in in_copies:
        copy.start()

    barrier = pltpu.get_barrier_semaphore()
    for d in range(1, n_chip):
        pl.semaphore_signal(
            barrier, inc=1, device_id={"ctx": chip_at(d) * 2 + core}, device_id_type=MESH
        )
    pl.semaphore_signal(barrier, inc=1, device_id={"ctx": sib}, device_id_type=MESH)

    pl.semaphore_signal(barrier, inc=1, device_id={"exp": partner}, device_id_type=MESH)

    @pl.when(inner == 1)
    def _():
        pl.semaphore_signal(barrier, inc=1, device_id={"exp": across}, device_id_type=MESH)

    pl.semaphore_wait(barrier, n_chip + 1 + inner)

    def raw_copy(src, s, send_sem, to):
        return pltpu.make_async_remote_copy(
            src_ref=src,
            dst_ref=raw.at[s],
            send_sem=send_sem,
            recv_sem=raw_recv.at[s],
            device_id={"exp": to},
            device_id_type=MESH,
        )

    own_copy = raw_copy(moe_ref, z, own_send, toward)
    own_copy.start()
    part = width // 2
    low, high = pl.ds(0, part), pl.ds(part, part)

    def side_copy(s):
        return pltpu.make_async_remote_copy(
            src_ref=moe_ref.at[:, low],
            dst_ref=raw.at[s, :, low],
            send_sem=side_send,
            recv_sem=raw_recv.at[s],
            device_id={"exp": partner},
            device_id_type=MESH,
        )

    @pl.when(inner == 1)
    def _():
        side_copy(z).start()

    relay_copy = raw_copy(raw.at[partner], partner, relay_send, across)

    w_copies = [
        pltpu.make_async_copy(w_hbm.at[0, :, pl.ds(i * width, width)], wbuf.at[i], w_sem.at[i])
        for i in range(n_z)
    ]
    for copy in w_copies:
        copy.start()

    def chunk_at(i):
        return 1 + i + upper_half * (1 - 2 * i) if i else z

    def forward_copy(i):
        s = chunk_at(i)
        return raw_copy(raw.at[s], s, fwd_send.at[i], partner)

    ids = ids_ref[...]
    gates = gate_ref[...]
    expert = lax.broadcasted_iota(jnp.int32, (8, length), 0)
    first, second = ids[0:1, :] == expert, ids[1:2, :] == expert
    named_row = (first | second).astype(jnp.float32)
    weight_row = jnp.where(first, gates[0:1, :], 0.0) + jnp.where(second, gates[1:2, :], 0.0)
    t_row = lax.broadcasted_iota(jnp.int32, (length, length), 0)
    t_col = lax.broadcasted_iota(jnp.int32, (length, length), 1)
    earlier = (t_row < t_col).astype(jnp.float32)
    rank_row = mm(named_row, earlier, NN)
    slot = lax.broadcasted_iota(jnp.int32, (cap, length), 0).astype(jnp.float32)
    for e in range(n_chip):
        hit = (rank_row[e : e + 1, :] == slot) & (named_row[e : e + 1, :] > 0.5)
        table[e] = hit.astype(jnp.float32).astype(jnp.bfloat16)
        gate = jnp.sum(jnp.where(hit, weight_row[e : e + 1, :], 0.0), axis=1, keepdims=True)
        slot_gate[e] = jnp.broadcast_to(gate, (cap, 128))
    for d in range(n_chip):
        near_table[pl.ds(d * cap, cap), :] = table[chip_at(d)]

    def block_of(s, b, i):
        return rows.at[s, b, :, low] if i == n_z - 1 else rows.at[s, b]

    def sent(i, d):
        return sendbuf.at[i, d - 1, :, low] if i == n_z - 1 else sendbuf.at[i, d - 1]

    def xy_copy(i, s, d):
        return pltpu.make_async_remote_copy(
            src_ref=sent(i, d),
            dst_ref=block_of(s, c, i),
            send_sem=xy_send.at[i, d],
            recv_sem=xy_recv.at[s, chip],
            device_id={"ctx": chip_at(d) * 2 + core},
            device_id_type=MESH,
        )

    def xy_arrival(i, s, d):
        source = chip_at(d)
        return pltpu.make_async_remote_copy(
            src_ref=sent(i, d),
            dst_ref=block_of(s, source * 2 + core, i),
            send_sem=xy_send.at[i, d],
            recv_sem=xy_recv.at[s, source],
            device_id={"ctx": source * 2 + core},
            device_id_type=MESH,
        )

    def sib_copy(s, d):
        block = rows.at[s, chip_at(d) * 2 + core]
        return pltpu.make_async_remote_copy(
            src_ref=block,
            dst_ref=block,
            send_sem=sib_send.at[s, d],
            recv_sem=sib_recv.at[s, d],
            device_id={"ctx": sib},
            device_id_type=MESH,
        )

    def sib_arrival(s, d):
        block = rows.at[s, chip_at(d) * 2 + 1 - core]
        return pltpu.make_async_remote_copy(
            src_ref=block,
            dst_ref=block,
            send_sem=sib_send.at[s, d],
            recv_sem=sib_recv.at[s, d],
            device_id={"ctx": sib},
            device_id_type=MESH,
        )

    def zp_copy(s, d):
        block = rows.at[s, chip_at(d) * 2 + core, :, high]
        return pltpu.make_async_remote_copy(
            src_ref=block,
            dst_ref=block,
            send_sem=zp_send.at[d],
            recv_sem=zp_recv.at[d],
            device_id={"exp": partner},
            device_id_type=MESH,
        )

    def take(i):
        forward_copy(i).wait_recv()

        @pl.when(inner == 1)
        def _():
            forward_copy(i).start()

    def route_chunk(i):
        half_only = i == n_z - 1
        s = partner if half_only else chunk_at(i)
        step = part // 2 if (part // 2) % 128 == 0 else part
        for at in range(0, part if half_only else width, step):
            cols = pl.ds(at, step)
            picked = mm(near_table[...], raw[s, :, cols], NN)
            for d in range(n_chip):
                gate = slot_gate[chip_at(d)][:, 0:1]
                routed = (picked[d * cap : (d + 1) * cap, :] * gate).astype(jnp.bfloat16)
                if d:
                    sendbuf[i, d - 1, :, cols] = routed
                else:
                    rows[s, c, :, cols] = routed
        for d in range(1, n_chip):
            xy_copy(i, s, d).start()
        if not half_only:
            sib_copy(s, 0).start()

    def pass_on(i):
        s = chunk_at(i)
        for d in range(1, n_chip):
            xy_arrival(i, s, d).wait_recv()
            sib_copy(s, d).start()

    def hid_copy(j):
        return pltpu.make_async_copy(
            hid.at[j],
            hid_hbm.at[0, pl.ds(pl.multiple_of(j * 2 * cap, 2 * cap), 2 * cap), :],
            hid_sem.at[j],
        )

    def multiply(s, first=False, last=False):
        if first:
            for copy in w_copies:
                copy.wait()

        def tile(j):
            left = rows[s, pl.ds(2 * j, 2)].reshape(2 * cap, width)
            total = mm(left, wbuf[s], NT)
            if not first:
                total = total + acc[j]
            if last:
                hid[j] = total.astype(jnp.bfloat16)
                hid_copy(j).start()
            else:
                acc[j] = total

        for d in range(n_chip):
            sib_arrival(s, d).wait_recv()
            tile(chip_at(d))

    moe_copy.wait()
    route_chunk(0)

    log_decay = ld_ref[...]
    highest = lax.Precision.HIGHEST
    lower = (t_row >= t_col).astype(jnp.float32)
    upper = (t_row <= t_col).astype(jnp.float32)
    running = mm(lower, log_decay, NT, highest)
    running_t = mm(log_decay, upper, NN, highest)
    closing = mm(log_decay, jnp.ones((length, size), jnp.float32), NN, highest)
    for h in range(heads):
        run_col[h] = jnp.broadcast_to(running[:, h : h + 1], (length, size))
        run_row[h] = jnp.broadcast_to(running_t[h : h + 1, :], (8, length))
        close_row[h] = jnp.broadcast_to(closing[h : h + 1, :], (8, size))
        own_decay[h] = jnp.broadcast_to(jnp.exp(closing[h : h + 1, :]), (8, size))

    group = 4 if heads % 4 == 0 else 2

    def per_head(body):
        def turn(i, carry):
            for u in range(group):
                h = i * group + u
                body(h, pl.ds(pl.multiple_of(h * size, size), size))
            return carry

        lax.fori_loop(0, heads // group, turn, 0)

    def block_states(h, cols):
        along = run_col[h]
        until = jnp.exp(close_row[h][0:1, :] - along)
        since = jnp.exp(along)
        key_high, key_low = split_bf16(k_ref[:, cols].astype(jnp.float32) * until)
        query_high, query_low = split_bf16(q_ref[:, cols].astype(jnp.float32) * since)
        value, grad = v_ref[:, cols], g_ref[:, cols]
        state[0, h] = mm(key_high, value, TN) + mm(key_low, value, TN)
        state[1, h] = mm(query_high, grad, TN) + mm(query_low, grad, TN)

    for copy in in_copies:
        copy.wait()
    per_head(block_states)

    def level(index, src, dst, peer):
        return pltpu.make_async_remote_copy(
            src_ref=src,
            dst_ref=dst,
            send_sem=lvl_send.at[index],
            recv_sem=lvl_recv.at[index],
            device_id={"ctx": peer},
            device_id_type=MESH,
        )

    core_state = level(0, state, sib_state, sib)
    core_decay = level(1, own_decay, sib_decay, sib)
    x_state = level(2, chip_state, far_state, xpart)
    x_decay = level(3, chip_decay, far_decay, xpart)
    y_copy = level(4, pair_state.at[ybit], y_state, ypart)
    outer_copy = level(5, outer.at[core], outer.at[core], sib)
    outer_arrival = level(5, outer.at[1 - core], outer.at[1 - core], sib)
    core_state.start()
    core_decay.start()

    def local_parts(h, cols):
        mask = causal_mask(length)
        spread = run_col[h] - run_row[h][0:1, :]
        weights = jnp.where(mask, jnp.exp(jnp.where(mask, spread, 0.0)), 0.0)
        query, key, value, grad = q_ref[:, cols], k_ref[:, cols], v_ref[:, cols], g_ref[:, cols]
        grad_scores = (mm(grad, value, NT) * weights).astype(jnp.bfloat16)
        scores = (mm(query, key, NT) * weights).astype(jnp.bfloat16)
        local[0, :, cols] = mm(grad_scores, key, NN)
        local[1, :, cols] = mm(grad_scores, query, TN)
        local[2, :, cols] = mm(scores, grad, TN)

    @pl.when(inner == 1)
    def _():
        relay_copy.wait_recv()
        relay_copy.start()

    @pl.when(inner == 0)
    def _():
        side_copy(partner).wait_recv()

    route_chunk(n_z - 1)

    core_state.wait_recv()
    core_decay.wait_recv()
    chip_decay[...] = own_decay[...] * sib_decay[...]

    def chip_totals(j, carry):
        h = core * half + j
        mine, theirs = own_decay[h][0:1, :], sib_decay[h][0:1, :]
        s_mine, s_sib = state[0, h], sib_state[0, h]
        g_mine, g_sib = state[1, h], sib_state[1, h]
        first_core = core == 0
        chip_state[0, j] = jnp.where(
            first_core, s_sib + theirs * s_mine, s_mine + mine * s_sib
        ).astype(jnp.bfloat16)
        chip_state[1, j] = jnp.where(
            first_core, g_mine + mine * g_sib, g_sib + theirs * g_mine
        ).astype(jnp.bfloat16)
        return carry

    lax.fori_loop(0, half, chip_totals, 0)
    x_state.start()
    x_decay.start()

    take(1)
    route_chunk(1)
    pass_on(0)

    def send_high():
        for d in range(n_chip):
            zp_copy(z, d).start()

    send_high()

    @pl.when(inner == 1)
    def _():
        forward_copy(2).wait_recv()
        forward_copy(2).start()

    per_head(local_parts)

    @pl.when(inner == 0)
    def _():
        forward_copy(2).wait_recv()

    route_chunk(2)
    multiply(z, first=True)

    x_state.wait_recv()
    x_decay.wait_recv()

    def pair_totals(j, carry):
        h = core * half + j
        mine, theirs = chip_decay[h][0:1, :], far_decay[h][0:1, :]
        s_mine, s_far = chip_state[0, j].astype(jnp.float32), far_state[0, j].astype(jnp.float32)
        g_mine, g_far = chip_state[1, j].astype(jnp.float32), far_state[1, j].astype(jnp.float32)
        first_x = xbit == 0
        pair_state[0, j] = jnp.where(
            first_x, s_far + theirs * s_mine, s_mine + mine * s_far
        ).astype(jnp.bfloat16)
        pair_state[1, j] = jnp.where(
            first_x, g_mine + mine * g_far, g_far + theirs * g_mine
        ).astype(jnp.bfloat16)
        return carry

    lax.fori_loop(0, half, pair_totals, 0)
    y_copy.start()

    pass_on(1)
    multiply(chunk_at(1))

    y_copy.wait_recv()

    def outer_states(j, carry):
        h = core * half + j
        theirs = far_decay[h][0:1, :]
        from_y = y_state[j].astype(jnp.float32)
        zero = jnp.zeros_like(from_y)
        y_prefix = jnp.where(ybit == 1, from_y, zero)
        y_suffix = jnp.where(ybit == 0, from_y, zero)
        s_far, g_far = far_state[0, j].astype(jnp.float32), far_state[1, j].astype(jnp.float32)
        outer[core, 0, j] = jnp.where(xbit == 1, s_far + theirs * y_prefix, y_prefix)
        outer[core, 1, j] = jnp.where(xbit == 0, g_far + theirs * y_suffix, y_suffix)
        return carry

    lax.fori_loop(0, half, outer_states, 0)
    outer_copy.start()

    outer_arrival.wait_recv()

    def finish(h, cols):
        along = run_col[h]
        until = jnp.exp(close_row[h][0:1, :] - along)
        since = jnp.exp(along)
        theirs = sib_decay[h][0:1, :]
        side, j = h // half, h % half
        before, after = outer[side, 0, j], outer[side, 1, j]
        prefix = jnp.where(core == 1, sib_state[0, h] + theirs * before, before)
        suffix = jnp.where(core == 0, sib_state[1, h] + theirs * after, after)
        prefix_high, prefix_low = split_bf16(prefix)
        suffix_high, suffix_low = split_bf16(suffix)
        key, value, grad = k_ref[:, cols], v_ref[:, cols], g_ref[:, cols]
        query_part = mm(grad, prefix_high, NT) + mm(grad, prefix_low, NT)
        key_part = mm(value, suffix_high, NT) + mm(value, suffix_low, NT)
        value_part = mm(key, suffix_high, NN) + mm(key, suffix_low, NN)
        grads[0, :, cols] = (local[0, :, cols] + since * query_part).astype(jnp.bfloat16)
        grads[1, :, cols] = (local[1, :, cols] + until * key_part).astype(jnp.bfloat16)
        grads[2, :, cols] = (local[2, :, cols] + until * value_part).astype(jnp.bfloat16)

    per_head(finish)
    out_copies = [
        pltpu.make_async_copy(grads.at[i], dst, out_sem.at[i])
        for i, dst in enumerate((qg_hbm, kg_hbm, vg_hbm))
    ]
    for copy in out_copies:
        copy.start()
    pass_on(2)
    multiply(chunk_at(2))
    for d in range(n_chip):
        if d:
            xy_arrival(n_z - 1, partner, d).wait_recv()
        zp_copy(partner, d).wait_recv()
        sib_copy(partner, d).start()
    multiply(partner, last=True)
    for copy in out_copies:
        copy.wait()
    for j in range(n_chip):
        hid_copy(j).wait()

    own_copy.wait_send()

    @pl.when(inner == 1)
    def _():
        relay_copy.wait_send()
        side_copy(z).wait_send()
        for i in range(1, n_z - 1):
            forward_copy(i).wait_send()

    for i in range(n_z - 1):
        s = chunk_at(i)
        for d in range(1, n_chip):
            xy_copy(i, s, d).wait_send()
        for d in range(n_chip):
            sib_copy(s, d).wait_send()
    for d in range(1, n_chip):
        xy_copy(n_z - 1, partner, d).wait_send()
    for d in range(n_chip):
        zp_copy(z, d).wait_send()
        sib_copy(partner, d).wait_send()
    for copy in (core_state, core_decay, x_state, x_decay, y_copy, outer_copy):
        copy.wait_send()


def hand_over(*refs):
    sources, results, stages, in_sem, out_sem = refs[:4], refs[4:8], refs[8:12], refs[12], refs[13]
    pulls = [pltpu.make_async_copy(sources[i], stages[i], in_sem.at[i]) for i in range(4)]
    pushes = [pltpu.make_async_copy(stages[i], results[i], out_sem.at[i]) for i in range(4)]
    for pull in pulls:
        pull.start()
    for pull, push in zip(pulls, pushes):
        pull.wait()
        push.start()
    for push in pushes:
        push.wait()


def fused(
    queries, keys, values, out_grad, log_decay, moe_grad, expert_ids, gate_weights, down_weight
):
    n_ctx, n_z = lax.axis_size("ctx"), lax.axis_size("exp")
    n_chip = n_ctx // 2
    length, heads = log_decay.shape
    width = moe_grad.shape[1]
    size = queries.shape[1] // heads
    cap = 5 * length // (2 * n_chip)
    half = heads // 2
    hidden = down_weight.shape[1]
    bf16, f32 = jnp.bfloat16, jnp.float32
    dma = pltpu.SemaphoreType.DMA
    vmem = pl.BlockSpec(memory_space=pltpu.VMEM)
    hbm = pl.BlockSpec(memory_space=pl.ANY)
    decay = pltpu.VMEM((heads, 8, size), f32)
    scratch = [
        *[pltpu.VMEM((length, heads * size), bf16)] * 4,
        pltpu.VMEM((3, length, heads * size), bf16),
        pltpu.VMEM((n_chip, 2 * cap, hidden), bf16),
        pltpu.VMEM((n_z, hidden, width), bf16),
        pltpu.VMEM((n_z, length, width), bf16),
        pltpu.VMEM((n_z, n_chip - 1, cap, width), bf16),
        pltpu.VMEM((n_z, n_ctx, cap, width), bf16),
        pltpu.VMEM((n_chip, 2 * cap, hidden), f32),
        pltpu.VMEM((n_chip, cap, length), bf16),
        pltpu.VMEM((n_chip * cap, length), bf16),
        pltpu.VMEM((n_chip, cap, 128), f32),
        pltpu.VMEM((heads, length, size), f32),
        pltpu.VMEM((heads, 8, length), f32),
        decay,
        decay,
        decay,
        decay,
        decay,
        pltpu.VMEM((2, heads, size, size), f32),
        pltpu.VMEM((2, heads, size, size), f32),
        pltpu.VMEM((2, half, size, size), bf16),
        pltpu.VMEM((2, half, size, size), bf16),
        pltpu.VMEM((2, half, size, size), bf16),
        pltpu.VMEM((half, size, size), bf16),
        pltpu.VMEM((2, 2, half, size, size), f32),
        pltpu.VMEM((3, length, width), f32),
        dma((4,)),
        dma((3,)),
        dma((n_chip,)),
        dma,
        dma((n_z,)),
        dma,
        dma,
        dma,
        dma((n_z - 1,)),
        dma((n_z,)),
        dma((n_z, n_chip)),
        dma((n_z, n_chip)),
        dma((n_chip,)),
        dma((n_chip,)),
        dma((n_z, n_chip)),
        dma((n_z, n_chip)),
        dma((6,)),
        dma((6,)),
    ]
    flat = jax.ShapeDtypeStruct((length, heads * size), bf16)
    results = pl.pallas_call(
        functools.partial(fused_kernel, (n_z, n_chip, cap, heads, size)),
        out_shape=(
            flat,
            flat,
            flat,
            jax.ShapeDtypeStruct((1, n_ctx * cap, hidden), bf16),
        ),
        in_specs=[hbm] * 4 + [vmem, hbm, vmem, vmem, hbm],
        out_specs=(hbm,) * 4,
        scratch_shapes=scratch,
        compiler_params=pltpu.CompilerParams(
            collective_id=0, has_side_effects=True, vmem_limit_bytes=60 * 2**20
        ),
    )(
        queries,
        keys,
        values,
        out_grad,
        log_decay.T,
        moe_grad,
        expert_ids.T,
        gate_weights.T,
        down_weight,
    )
    return pl.pallas_call(
        hand_over,
        out_shape=tuple(jax.ShapeDtypeStruct(x.shape, x.dtype) for x in results),
        in_specs=[hbm] * 4,
        out_specs=(hbm,) * 4,
        scratch_shapes=[*[pltpu.VMEM(x.shape, x.dtype) for x in results], dma((4,)), dma((4,))],
        compiler_params=pltpu.CompilerParams(vmem_limit_bytes=60 * 2**20),
    )(*results)


def body(
    queries, keys, values, out_grad, log_decay, moe_grad, expert_ids, gate_weights, down_weight
):
    n_ctx, n_z = lax.axis_size("ctx"), lax.axis_size("exp")
    length, heads = log_decay.shape
    cap = 5 * length // n_ctx
    args = (
        queries, keys, values, out_grad, log_decay, moe_grad, expert_ids, gate_weights, down_weight
    )
    size = queries.shape[1] // heads
    fits = (
        n_ctx == 8
        and n_z == 4
        and cap % 16 == 0
        and size == 128
        and length == 128
        and heads % 2 == 0
        and moe_grad.shape[1] % 256 == 0
        and queries.shape[1] == moe_grad.shape[1]
    )
    return fused(*args) if fits else per_device(*args)


def solution(mesh):
    in_specs = (
        P("ctx", "exp"),
        P("ctx", "exp"),
        P("ctx", "exp"),
        P("ctx", "exp"),
        P("ctx", "exp"),
        P("ctx", "exp"),
        P("ctx", None),
        P("ctx", None),
        P("ctx", "exp", None),
    )
    out_specs = (P("ctx", "exp"), P("ctx", "exp"), P("ctx", "exp"), P("ctx", None, "exp"))
    return jax.shard_map(
        body, mesh=mesh, in_specs=in_specs, out_specs=out_specs, check_vma=False
    )
```
